1024 devices in a mesh: grp: 8 (over y), reg: 128 (over z, x, core).
Axes of the slice: x: 8, y: 8, z: 8, core: 2. Of those that a mesh axis runs over, the one named last changes fastest.
Arguments:
- field: bfloat16 [128, 1024, 1024], P(None, 'reg', 'grp'), may hold values from -6 to 6
- send_pick: int32 [16384], P(('grp', 'reg')), may hold values from 0 to 7
- blk_src: int32 [32768], P(('grp', 'reg')), may hold values from 0 to 47, as said below
- blk_ocn: int32 [32768], P(('grp', 'reg')), may hold values from 0 to 4, as said below
- blk_weight: bfloat16 [32768, 384, 128], P(('grp', 'reg')), may hold values from -0.3125 to 0.3125
Outputs:
- remapped: bfloat16 [128, 524288], P(None, ('grp', 'reg'))
The draws below stay inside these ranges and needn't reach their ends.
Inputs may be any that keep to these rules, and one draw needn't show every extreme that they name: `blk_src`: slots 0 to 15 are the lower region's pool, the next 16 the device's own, the last 16 the upper region's. Each device's blocks name at most 4 distinct slots of each neighbouring region's pool, exactly 4 on every device. `blk_ocn`: the value 4 marks an empty slot; every device has one or more empty slots.
All inputs are finite; a program needn't handle non-finite values.
Results may differ from the reference program's by a relative error of at most 0.0041.
Values may be sent and summed in bfloat16 or wider, within the bound.
A program may use at most 32 MiB of HBM per device.

```python
import jax
import jax.numpy as jnp
from jax import lax

CH = 128
TILE = 128
CX = 8
CAP = 2
NBR = 4
OCN = 4
BLK = 32
NX = 1024
NY = 1024
N_GRP = 8
N_REG = 128
DEVICES = 1024


def block_order(key):
    keys = jax.random.split(jax.random.fold_in(key, 7), DEVICES)
    return jax.vmap(lambda single: jax.random.permutation(single, BLK))(keys)


def draw_send_pick(key, part):
    key = jax.random.fold_in(key, 17)

    def one_device(single):
        first_key, second_key, third_key = jax.random.split(single, 3)
        covered = jax.random.permutation(first_key, CX)
        others = jax.random.randint(second_key, (N_GRP * CAP - CX,), 0, CX)
        joined = jnp.concatenate([covered, others]).astype(jnp.int32)
        return jax.random.permutation(third_key, joined)
    return jax.vmap(one_device)(jax.random.split(key, DEVICES)).reshape(-1).astype(jnp.int32)


def draw_blk_src(key, part):
    order = block_order(key)
    key = jax.random.fold_in(key, 11)
    pool_size = N_GRP * CAP
    cover = 2 * NBR + pool_size

    def one_device(single, place):
        first_key, second_key, third_key = jax.random.split(single, 3)
        lower = jax.random.permutation(first_key, pool_size)[:NBR]
        upper = jax.random.permutation(second_key, pool_size)[:NBR] + 2 * pool_size
        own_slots = jnp.arange(pool_size, dtype=jnp.int32) + pool_size
        candidates = jnp.concatenate([lower, upper, own_slots]).astype(jnp.int32)
        extra = candidates[jax.random.randint(third_key, (BLK - cover,), 0, cover)]
        content = jnp.concatenate([candidates, extra]).astype(jnp.int32)
        return content[place]
    return jax.vmap(one_device)(jax.random.split(key, DEVICES), order).reshape(-1).astype(jnp.int32)


def draw_blk_ocn(key, part):
    order = block_order(key)
    key = jax.random.fold_in(key, 13)
    cover = 2 * NBR + N_GRP * CAP

    def one_device(single, place):
        first_key, second_key = jax.random.split(single)
        live = jax.random.randint(first_key, (), cover, BLK)
        target = jax.random.randint(second_key, (BLK,), 0, OCN)
        return jnp.where(place < live, target, OCN).astype(jnp.int32)
    return jax.vmap(one_device)(jax.random.split(key, DEVICES), order).reshape(-1).astype(jnp.int32)


def shard_levels(key, extent, cuts, smallest, high):
    gain, own = 1.0, jax.random.fold_in(key, 6)
    for dim, shards_of in cuts:
        draws = jnp.exp(jax.random.uniform(jax.random.fold_in(own, dim), (shards_of,), jnp.float32, smallest / len(cuts), high / len(cuts)))
        gain = gain * jnp.repeat(draws, extent[dim] // shards_of).reshape([-1 if axis == dim else 1 for axis in range(len(extent))])
    return gain


def normal_values(stream_key, dims, spread, bound, cuts=(), kind=jnp.bfloat16):
    drawn = jax.random.normal(stream_key, dims, jnp.float32) * spread
    if len(cuts) > 0:
        drawn = shard_levels(stream_key, dims, cuts, -0.22, 0.18) * drawn
    return jnp.clip(drawn, min=-bound, max=bound).astype(kind)


def setup_inputs(seed: int = 0) -> dict:
    key_list = jax.random.split(jax.random.key(seed), 6)
    return {
        "field": normal_values(key_list[0], (CH, NX, NY), 1.0, 6.0, ((1, 128), (2, 8))),
        "send_pick": draw_send_pick(jax.random.fold_in(key_list[5], 71), 0),
        "blk_src": draw_blk_src(jax.random.fold_in(key_list[5], 71), 0),
        "blk_ocn": draw_blk_ocn(jax.random.fold_in(key_list[5], 71), 0),
        "blk_weight": normal_values(key_list[4], (DEVICES * BLK, 3 * TILE, TILE), (3 * TILE) ** -0.5, 0.3125, ((0, 1024),)),
    }


def gradients(field):
    padded = jnp.pad(field.astype(jnp.float32), ((0, 0), (1, 1), (1, 1)))
    grad_x = ((padded[:, 2:, 1:-1] - padded[:, :-2, 1:-1]) * 0.5).astype(jnp.bfloat16)
    grad_y = ((padded[:, 1:-1, 2:] - padded[:, 1:-1, :-2]) * 0.5).astype(jnp.bfloat16)
    return grad_x, grad_y


def as_tiles(array):
    shaped = array.reshape(CH, N_REG, CX, N_GRP, TILE)
    return jnp.transpose(shaped, (3, 1, 2, 0, 4))


def reference(field, send_pick, blk_src, blk_ocn, blk_weight):
    grad_x, grad_y = gradients(field)
    tiles = jnp.concatenate([as_tiles(field), as_tiles(grad_x), as_tiles(grad_y)], axis=4)
    picks = send_pick.reshape(N_GRP, N_REG, N_GRP, CAP)
    sources_all = blk_src.reshape(N_GRP * N_REG, BLK)
    targets_all = blk_ocn.reshape(N_GRP * N_REG, BLK)
    weights_all = blk_weight.reshape(N_GRP * N_REG, BLK, 3 * TILE, TILE)
    senders = jnp.arange(N_GRP, dtype=jnp.int32)[:, None]
    ocean_ids = jnp.arange(OCN, dtype=jnp.int32)[:, None]

    def one_device(items):
        device, sources, targets, weights = items
        group = device // N_REG
        region = device % N_REG
        pieces = []
        for offset in (-1, 0, 1):
            near = region + offset
            inside = ((near >= 0) & (near < N_REG)).astype(jnp.bfloat16)
            near = jnp.clip(near, 0, N_REG - 1).astype(jnp.int32)
            chosen = picks[:, near, group, :]
            block = tiles[senders, near, chosen]
            pieces.append((block * inside).reshape(N_GRP * CAP, CH, 3 * TILE))
        extended = jnp.concatenate(pieces, axis=0)
        gathered = extended[sources].astype(jnp.float32)
        partial_value = jnp.einsum("bcs,bst->bct", gathered, weights.astype(jnp.float32), precision=lax.Precision.HIGHEST)
        onehot = (targets[None, :] == ocean_ids).astype(jnp.float32)
        return jnp.einsum("ob,bct->oct", onehot, partial_value, precision=lax.Precision.HIGHEST)

    devices = jnp.arange(N_GRP * N_REG, dtype=jnp.int32)
    result = lax.map(one_device, (devices, sources_all, targets_all, weights_all))
    result = jnp.transpose(result, (2, 0, 1, 3)).reshape(CH, N_GRP * N_REG * OCN * TILE)
    return result.astype(jnp.bfloat16)
```

```python
import functools

import jax
import jax.numpy as jnp
from jax import lax
from jax.experimental import pallas as pl
from jax.experimental.pallas import tpu as pltpu
from jax.sharding import PartitionSpec as P

MESH = pl.DeviceIdType.MESH
OCN = 4
CAP = 2
NBR = 4
G = 8
LANES = 128
ORDER = (0, 3, 1, 2)
RIGHT_LAST = (0, 1)
LEFT_LAST = (3, 2)


def distinct(src_ref, low):
    found = [jnp.int32(0)] * NBR
    count = jnp.int32(0)
    for b in range(src_ref.shape[0]):
        slot = src_ref[b] - low
        fresh = (slot >= 0) & (slot < 2 * G)
        for k in range(NBR):
            fresh = fresh & ((count <= k) | (found[k] != slot))
        for k in range(NBR):
            found[k] = jnp.where(fresh & (count == k), slot, found[k])
        count = count + fresh.astype(jnp.int32)
    return found


def kernel(regions, field_ref, pick_ref, src_ref, ocn_ref, w_hbm, out_ref,
           row0, row1, row2, row3, row4, row5, row6, row7, halos, pool, tiles, stage, weights, flat, meta, asked, meta_s, asked_s, place_s, diff, part,
           ring_send, ring_recv, meta_send, meta_recv, halo_send, halo_recv, ask_send, ask_recv,
           nbr_send, nbr_recv, local_sem, w_sem):
    me = lax.axis_index("grp")
    r = lax.axis_index("reg")
    rows = (row0, row1, row2, row3, row4, row5, row6, row7)
    cx = field_ref.shape[1]
    blocks = src_ref.shape[0]
    right, left = lax.rem(me + 1, G), lax.rem(me + G - 1, G)
    has_low, has_high = r > 0, r < regions - 1
    low, high = jnp.maximum(r - 1, 0), jnp.minimum(r + 1, regions - 1)

    def at(offset):
        return lax.rem(me + offset + G, G)

    barrier = pltpu.get_barrier_semaphore()
    for peer in (left, right):
        pl.semaphore_signal(barrier, inc=1, device_id=(peer, r), device_id_type=MESH)

    @pl.when(has_low)
    def _():
        pl.semaphore_signal(barrier, inc=1, device_id=(me, low), device_id_type=MESH)

    @pl.when(has_high)
    def _():
        pl.semaphore_signal(barrier, inc=1, device_id=(me, high), device_id_type=MESH)

    w_copy = pltpu.make_async_copy(w_hbm, weights, w_sem)
    w_copy.start()

    flat[...] = field_ref[...].astype(jnp.float32).reshape(flat.shape)
    for i in range(cx):
        row0[i] = flat[pl.ds(i, row0.shape[1], stride=cx), :].astype(jnp.bfloat16)

    wanted_low, wanted_high = distinct(src_ref, 0), distinct(src_ref, 4 * G)
    lane = lax.broadcasted_iota(jnp.int32, (8, LANES), 1)
    note = jnp.zeros((8, LANES), jnp.int32)
    for k in range(G * CAP):
        note = jnp.where(lane == k, pick_ref[k], note)
    for k in range(NBR):
        note = jnp.where(lane == G * CAP + k, wanted_low[k], note)
        note = jnp.where(lane == G * CAP + NBR + k, wanted_high[k], note)
    meta[me] = note
    for b in range(blocks):
        slot = src_ref[b]
        spot = jnp.int32(2 * G)
        for k in range(1, NBR):
            spot = jnp.where(slot == wanted_low[k], 2 * G + k, spot)
        upper = jnp.int32(2 * G + NBR)
        for k in range(1, NBR):
            upper = jnp.where(slot - 4 * G == wanted_high[k], 2 * G + NBR + k, upper)
        spot = jnp.where(slot >= 2 * G, slot - 2 * G, spot)
        place_s[b] = jnp.where(slot >= 4 * G, upper, spot)

    depth = lax.broadcasted_iota(jnp.int32, (3 * LANES, LANES), 0)
    column = lax.broadcasted_iota(jnp.int32, (3 * LANES, LANES), 1) + LANES
    whole = (jnp.where(depth == column + 1, 0.5, 0.0) - jnp.where(depth == column - 1, 0.5, 0.0)).astype(jnp.float32)
    diff[0] = jnp.where(depth >= LANES, whole, 0.0).astype(jnp.bfloat16)
    diff[1] = whole.astype(jnp.bfloat16)
    diff[2] = jnp.where(depth < 2 * LANES, whole, 0.0).astype(jnp.bfloat16)

    @pl.when(jnp.logical_not(has_low))
    def _():
        for d in range(G):
            halos[0, d] = jnp.zeros(halos.shape[2:], halos.dtype)
        for k in range(NBR):
            tiles[2 * G + k] = jnp.zeros(tiles.shape[1:], tiles.dtype)

    @pl.when(jnp.logical_not(has_high))
    def _():
        for d in range(G):
            halos[1, d] = jnp.zeros(halos.shape[2:], halos.dtype)
        for k in range(NBR):
            tiles[2 * G + NBR + k] = jnp.zeros(tiles.shape[1:], tiles.dtype)

    pl.semaphore_wait(barrier, 2 + has_low.astype(jnp.int32) + has_high.astype(jnp.int32))

    def chunk(offset, c):
        return rows[offset % G].at[pl.ds(2 * c, 2)]

    def ring(way, step, c):
        sign = -1 if way == 0 else 1
        return pltpu.make_async_remote_copy(
            src_ref=chunk(sign * (step - 1), c), dst_ref=chunk(sign * step, c),
            send_sem=ring_send.at[way, step - 1, c], recv_sem=ring_recv.at[way, step - 1, c],
            device_id=(right if way == 0 else left, r), device_id_type=MESH)

    def ring_arrived(way, step, c):
        ring(way, step, c).wait_recv()

    def note_copy(way, step):
        h = at(-(step - 1)) if way == 0 else at(step - 1)
        return pltpu.make_async_remote_copy(
            src_ref=meta.at[h], dst_ref=meta.at[h],
            send_sem=meta_send.at[way, step - 1], recv_sem=meta_recv.at[way, step - 1],
            device_id=(right if way == 0 else left, r), device_id_type=MESH)

    def note_arrived(way, step):
        h = at(-step) if way == 0 else at(step)
        pltpu.make_async_remote_copy(
            src_ref=meta.at[h], dst_ref=meta.at[h],
            send_sem=meta_send.at[way, step - 1], recv_sem=meta_recv.at[way, step - 1],
            device_id=(right if way == 0 else left, r), device_id_type=MESH).wait_recv()

    def to_smem(offset):
        h = at(offset)
        return pltpu.make_async_copy(meta.at[h], meta_s.at[h], local_sem.at[offset % G])

    def halo(way, offset):
        return pltpu.make_async_remote_copy(
            src_ref=rows[offset % G].at[cx - 1 if way == 0 else 0], dst_ref=halos.at[way, offset % G],
            send_sem=halo_send.at[way, offset % G], recv_sem=halo_recv.at[way, offset % G],
            device_id=(me, high if way == 0 else low), device_id_type=MESH)

    def send_halo(way, offset):
        @pl.when(has_high if way == 0 else has_low)
        def _():
            halo(way, offset).start()

    def halos_arrived(offset):
        @pl.when(has_low)
        def _():
            halo(0, offset).wait_recv()

        @pl.when(has_high)
        def _():
            halo(1, offset).wait_recv()

    def ask(way):
        return pltpu.make_async_remote_copy(
            src_ref=meta.at[me], dst_ref=asked.at[way],
            send_sem=ask_send.at[way], recv_sem=ask_recv.at[way],
            device_id=(me, high if way == 0 else low), device_id_type=MESH)

    def neighbour_tile(way, k):
        return pltpu.make_async_remote_copy(
            src_ref=stage.at[way * NBR + k], dst_ref=tiles.at[2 * G + way * NBR + k],
            send_sem=nbr_send.at[way, k], recv_sem=nbr_recv.at[way, k],
            device_id=(me, high if way == 0 else low), device_id_type=MESH)

    for way in range(2):
        note_copy(way, 1).start()
    for c in ORDER:
        for way in range(2):
            ring(way, 1, c).start()
    to_smem(0).start()

    @pl.when(has_high)
    def _():
        ask(0).start()

    @pl.when(has_low)
    def _():
        ask(1).start()

    for way in range(2):
        send_halo(way, 0)

    def make_tiles(offset):
        halos_arrived(offset)
        to_smem(offset).wait()
        h = at(offset)
        here, before, after = rows[offset % G], rows[(offset - 1) % G], rows[(offset + 1) % G]
        kind = jnp.where(h == 0, 0, jnp.where(h == G - 1, 2, 1))
        for c in range(CAP):
            i = meta_s[h, 0, CAP * me + c]
            own = here[i]
            up = jnp.where(i == 0, halos[0, offset % G], here[jnp.maximum(i - 1, 0)]).astype(jnp.float32)
            down = jnp.where(i == cx - 1, halos[1, offset % G], here[jnp.minimum(i + 1, cx - 1)]).astype(jnp.float32)
            grad_x = ((down - up) * 0.5).astype(jnp.bfloat16)
            side = jnp.concatenate([before[i], own, after[i]], axis=1)
            grad_y = jnp.dot(side, diff[kind], preferred_element_type=jnp.float32).astype(jnp.bfloat16)
            whole = jnp.concatenate([own, grad_x, grad_y], axis=1)
            pool[CAP * h + c] = whole
            tiles[CAP * h + c] = whole

    for step in range(1, 5):
        both = step < 4
        note_arrived(0, step)
        if step < 4:
            note_copy(0, step + 1).start()
        to_smem(-step).start()
        if both:
            note_arrived(1, step)
            if step < 3:
                note_copy(1, step + 1).start()
            to_smem(step).start()
        right_order = ORDER if both else RIGHT_LAST
        left_order = ORDER if both else LEFT_LAST
        for c, d in zip(right_order, left_order):
            ring_arrived(0, step, c)
            if step < 3 or (step == 3 and c in RIGHT_LAST):
                ring(0, step + 1, c).start()
            if c == 0:
                send_halo(1, -step)
            if c == 3:
                send_halo(0, -step)
            ring_arrived(1, step, d)
            if step < 3 or (step == 3 and d in LEFT_LAST):
                ring(1, step + 1, d).start()
            if d == 0:
                send_halo(1, step)
            if d == 3:
                send_halo(0, step)
        if step == 1:
            make_tiles(0)
        else:
            make_tiles(-(step - 1))
            make_tiles(step - 1)
    make_tiles(4)

    def serve(way):
        arrived = ask(1 - way)
        arrived.wait_recv()
        to_scalar = pltpu.make_async_copy(asked.at[1 - way], asked_s.at[1 - way], local_sem.at[G + way])
        to_scalar.start()
        to_scalar.wait()
        for k in range(NBR):
            slot = asked_s[1 - way, 0, G * CAP + way * NBR + k]
            stage[way * NBR + k] = pool[slot]
            neighbour_tile(way, k).start()

    @pl.when(has_high)
    def _():
        serve(0)

    @pl.when(has_low)
    def _():
        serve(1)

    w_copy.wait()

    @pl.when(has_low)
    def _():
        for k in range(NBR):
            neighbour_tile(0, k).wait_recv()

    @pl.when(has_high)
    def _():
        for k in range(NBR):
            neighbour_tile(1, k).wait_recv()

    @pl.loop(0, blocks // 4)
    def _(quarter):
        for k in range(4):
            b = quarter * 4 + k
            part[b] = jnp.dot(tiles[place_s[b]], weights[b], preferred_element_type=jnp.float32)

    height = 16

    @pl.loop(0, part.shape[1] // height)
    def _(band):
        here = pl.ds(pl.multiple_of(band * height, height), height)
        sums = [jnp.zeros((height, LANES), jnp.float32) for _ in range(OCN)]
        for b in range(blocks):
            value = part[b, here, :]
            for t in range(OCN):
                sums[t] = sums[t] + value * (ocn_ref[b] == t).astype(jnp.float32)
        for t in range(OCN):
            out_ref[here, t * LANES:(t + 1) * LANES] = sums[t].astype(jnp.bfloat16)

    for step in range(1, 5):
        note_copy(0, step).wait_send()
        if step < 4:
            note_copy(1, step).wait_send()
        for c in ORDER if step < 4 else RIGHT_LAST:
            ring(0, step, c).wait_send()
        for c in ORDER if step < 4 else LEFT_LAST:
            ring(1, step, c).wait_send()

    for way, there in ((0, has_high), (1, has_low)):
        @pl.when(there)
        def _(way=way):
            ask(way).wait_send()
            for offset in range(G):
                halo(way, offset).wait_send()
            for k in range(NBR):
                neighbour_tile(way, k).wait_send()


def solution(mesh):
    regions = mesh.shape["reg"]

    def per_device(field, send_pick, blk_src, blk_ocn, blk_weight):
        channels, cx, cells = field.shape
        blocks = blk_src.shape[0]
        vmem = pl.BlockSpec(memory_space=pltpu.VMEM)
        smem = pl.BlockSpec(memory_space=pltpu.SMEM)
        dma = pltpu.SemaphoreType.DMA
        bf16, f32, i32 = jnp.bfloat16, jnp.float32, jnp.int32
        return pl.pallas_call(
            functools.partial(kernel, regions),
            out_shape=jax.ShapeDtypeStruct((channels, OCN * cells), bf16),
            in_specs=[vmem, smem, smem, smem, pl.BlockSpec(memory_space=pltpu.HBM)],
            out_specs=vmem,
            scratch_shapes=[
                *[pltpu.VMEM((cx, channels, cells), bf16) for _ in range(G)],
                pltpu.VMEM((2, G, channels, cells), bf16),
                pltpu.VMEM((G * CAP, channels, 3 * cells), bf16),
                pltpu.VMEM((G * CAP + 2 * NBR, channels, 3 * cells), bf16),
                pltpu.VMEM((2 * NBR, channels, 3 * cells), bf16),
                pltpu.VMEM((blocks, 3 * cells, cells), bf16),
                pltpu.VMEM((channels * cx, cells), f32),
                pltpu.VMEM((G, 8, LANES), i32),
                pltpu.VMEM((2, 8, LANES), i32),
                pltpu.SMEM((G, 8, LANES), i32),
                pltpu.SMEM((2, 8, LANES), i32),
                pltpu.SMEM((blocks,), i32),
                pltpu.VMEM((3, 3 * cells, cells), bf16),
                pltpu.VMEM((blocks, channels, cells), f32),
                dma((2, 4, 4)), dma((2, 4, 4)),
                dma((2, 4)), dma((2, 4)),
                dma((2, G)), dma((2, G)),
                dma((2,)), dma((2,)),
                dma((2, NBR)), dma((2, NBR)),
                dma((G + 2,)),
                dma,
            ],
            compiler_params=pltpu.CompilerParams(
                collective_id=0, has_side_effects=True, vmem_limit_bytes=40 * 1024 * 1024
            ),
            cost_estimate=pl.CostEstimate(
                flops=2 * blocks * channels * 3 * cells * cells, bytes_accessed=4 * 1024 * 1024, transcendentals=0
            ),
        )(field, send_pick, blk_src, blk_ocn, blk_weight)

    placed = (
        P(None, "reg", "grp"),
        P(("grp", "reg")),
        P(("grp", "reg")),
        P(("grp", "reg")),
        P(("grp", "reg"), None, None),
    )
    return jax.shard_map(
        per_device, mesh=mesh, in_specs=placed, out_specs=P(None, ("grp", "reg")), check_vma=False
    )
```

```python
import functools

import jax
import jax.numpy as jnp
from jax import lax
from jax.experimental import pallas as pl
from jax.experimental.pallas import tpu as pltpu
from jax.sharding import PartitionSpec as P

MESH = pl.DeviceIdType.MESH
OCN = 4
CAP = 2
NBR = 4
G = 8
LANES = 128
VMEM_LIMIT = 48 * 1024 * 1024
ORDER = (0, 3, 1, 2)
OWN = G * CAP
EARLY, LATE = OWN, OWN + 2 * NBR
SLOTS = LATE + 2 * CAP


def transposed(matrix, unit):
    return lax.dot_general(
        unit, matrix, (((1,), (1,)), ((), ())), preferred_element_type=jnp.float32
    ).astype(jnp.bfloat16)


def distinct(src_ref, low):
    found = [jnp.int32(0)] * NBR
    count = jnp.int32(0)
    for b in range(src_ref.shape[0]):
        slot = src_ref[b] - low
        fresh = (slot >= 0) & (slot < OWN)
        for k in range(NBR):
            fresh = fresh & ((count <= k) | (found[k] != slot))
        for k in range(NBR):
            found[k] = jnp.where(fresh & (count == k), slot, found[k])
        count = count + fresh.astype(jnp.int32)
    return found


def kernel(regions, field_hbm, pick_hbm, src_hbm, ocn_hbm, w_hbm, out_ref,
           field_ref, pick_ref, src_ref, ocn_ref,
           row0, row1, row2, row3, row5, row6, row7, halos, edges, wish, fringe,
           pass3, pass4, got3, got4, pool, tiles, stage, near, late, weights, flat,
           meta, asked, meta_s, asked_s, place_s, band, part, fringe_out,
           ring_send, ring_recv, pass_send, pass_recv, meta_send, meta_recv, edge_send, edge_recv,
           halo_send, halo_recv, ask_send, ask_recv, near_send, near_recv, fringe_send, fringe_recv,
           late_send, late_recv, local_sem, in_sem, w_sem):
    me = lax.axis_index("grp")
    r = lax.axis_index("reg")
    rows = {0: row0, 1: row1, 2: row2, 3: row3, -3: row5, -2: row6, -1: row7}
    channels, cx = field_ref.shape[:2]
    half = channels // 2
    first, second = pl.ds(0, half), pl.ds(half, half)
    raw_half = (first, second)
    blocks = src_ref.shape[0]
    f32, bf16 = jnp.float32, jnp.bfloat16
    right, left = lax.rem(me + 1, G), lax.rem(me + G - 1, G)
    has_low, has_high = r > 0, r < regions - 1
    low, high = jnp.maximum(r - 1, 0), jnp.minimum(r + 1, regions - 1)
    there = (has_high, has_low)

    def at(offset):
        return lax.rem(me + offset + G, G)

    def along(way):
        return (right if way == 0 else left, r)

    def across(way):
        return (me, high if way == 0 else low)

    def remote(source, target, send, receive, device):
        return pltpu.make_async_remote_copy(
            src_ref=source, dst_ref=target, send_sem=send, recv_sem=receive, device_id=device, device_id_type=MESH)

    arriving = [
        pltpu.make_async_copy(origin, here, in_sem.at[k])
        for k, (origin, here) in enumerate(
            ((field_hbm, field_ref), (pick_hbm, pick_ref), (src_hbm, src_ref), (ocn_hbm, ocn_ref)))
    ]
    for copy in arriving:
        copy.start()
    barrier = pltpu.get_barrier_semaphore()
    for way in range(2):
        pl.semaphore_signal(barrier, inc=1, device_id=along(way), device_id_type=MESH)

    for way in range(2):
        @pl.when(there[way])
        def _(way=way):
            pl.semaphore_signal(barrier, inc=1, device_id=across(way), device_id_type=MESH)

    w_copy = pltpu.make_async_copy(w_hbm, weights, w_sem)
    w_copy.start()

    fringe[...] = jnp.zeros(fringe.shape, bf16)
    for c in range(CAP):
        pool[CAP * at(4) + c] = jnp.zeros(pool.shape[1:], bf16)

    for way in range(2):
        @pl.when(jnp.logical_not(there[1 - way]))
        def _(way=way):
            for d in range(G):
                halos[way, d] = jnp.zeros(halos.shape[2:], bf16)
            for k in range(NBR):
                tiles[EARLY + way * NBR + k] = jnp.zeros(tiles.shape[1:], bf16)
            for c in range(CAP):
                tiles[LATE + way * CAP + c] = jnp.zeros(tiles.shape[1:], bf16)

    arriving[0].wait()
    flat[...] = field_ref[...].astype(f32).reshape(flat.shape)
    for i in range(cx):
        row0[i] = flat[pl.ds(i, channels, stride=cx), :].astype(bf16)

    pl.semaphore_wait(barrier, 2 + has_low.astype(jnp.int32) + has_high.astype(jnp.int32))

    def ring(way, step, c):
        sign = -1 if way == 0 else 1
        source = rows[sign * (step - 1)].at[pl.ds(2 * c, 2)]
        if step == 3:
            source = rows[sign * 2].at[pl.ds(2 * c, 2), raw_half[way]]
        return remote(source, rows[sign * step].at[pl.ds(2 * c, 2)],
                      ring_send.at[way, step - 1, c], ring_recv.at[way, step - 1, c], along(way))

    def passed(way, step):
        source, target = (pass3, got3) if step == 3 else (pass4, got4)
        return remote(source.at[way], target.at[way],
                      pass_send.at[way, step - 3], pass_recv.at[way, step - 3], along(way))

    def note_copy(way, step, receiving=False):
        sign = -1 if way == 0 else 1
        h = at(sign * (step if receiving else step - 1))
        return remote(meta.at[h], meta.at[h], meta_send.at[way, step - 1], meta_recv.at[way, step - 1], along(way))

    def edge_copy(way, step, receiving=False):
        sign = -1 if way == 0 else 1
        h = at(sign * (step if receiving else step - 1))
        return remote(edges.at[h], edges.at[h], edge_send.at[way, step - 1], edge_recv.at[way, step - 1], along(way))

    def to_smem(offset):
        h = at(offset)
        return pltpu.make_async_copy(meta.at[h], meta_s.at[h], local_sem.at[offset % G])

    def halo(way, offset):
        source = rows[offset].at[cx - 1 if way == 0 else 0]
        target = halos.at[way, offset % G]
        if abs(offset) == 3:
            target = halos.at[way, offset % G, first if offset < 0 else second]
        return remote(source, target, halo_send.at[way, offset % G], halo_recv.at[way, offset % G], across(way))

    def send_halo(way, offset):
        @pl.when(there[way])
        def _():
            halo(way, offset).start()

    def halos_arrived(offset):
        for way in range(2):
            @pl.when(there[1 - way])
            def _(way=way):
                halo(way, offset).wait_recv()

    def ask(way):
        return remote(wish, asked.at[way], ask_send.at[way], ask_recv.at[way], across(way))

    def near_copy(way, k):
        return remote(stage.at[way, k], near.at[way, k], near_send.at[way, k], near_recv.at[way, k], across(way))

    def fringe_copy(way):
        return remote(fringe_out.at[way], fringe.at[pl.ds(16 * way, 16)],
                      fringe_send.at[way], fringe_recv.at[way], across(way))

    def late_copy(way, chain):
        return remote(got4.at[chain], late.at[way, chain],
                      late_send.at[way, chain], late_recv.at[way, chain], across(way))

    for c in ORDER:
        for way in range(2):
            ring(way, 1, c).start()
        if c == 3:
            for way in range(2):
                send_halo(way, 0)

    for copy in arriving[1:]:
        copy.wait()
    lane = lax.broadcasted_iota(jnp.int32, (8, LANES), 1)
    note = jnp.zeros((8, LANES), jnp.int32)
    for k in range(OWN):
        note = jnp.where(lane == k, pick_ref[k], note)
    meta[me] = note
    line = lax.broadcasted_iota(jnp.int32, (16, LANES), 0)
    spot = lax.broadcasted_iota(jnp.int32, (16, LANES), 1)
    border = jnp.zeros((16, channels), f32)
    for i in range(cx):
        chosen = ((line == i) & (spot == 0)) | ((line == 8 + i) & (spot == LANES - 1))
        border = border + lax.dot_general(
            jnp.where(chosen, 1.0, 0.0).astype(bf16), row0[i], (((1,), (1,)), ((), ())), preferred_element_type=f32)
    edges[me] = border.astype(bf16)
    for way in range(2):
        note_copy(way, 1).start()
        edge_copy(way, 1).start()
    to_smem(0).start()

    wanted = (distinct(src_ref, 0), distinct(src_ref, 2 * OWN))
    request = jnp.zeros((8, LANES), jnp.int32)
    for way in range(2):
        for k in range(NBR):
            request = jnp.where(lane == way * NBR + k, wanted[way][k], request)
    wish[...] = request
    for way in range(2):
        @pl.when(there[way])
        def _(way=way):
            ask(way).start()
    far = CAP * at(4)
    for b in range(blocks):
        slot = src_ref[b]
        found = []
        for way in range(2):
            named = slot - 2 * OWN * way
            where = jnp.int32(EARLY + way * NBR)
            for k in range(1, NBR):
                where = jnp.where(named == wanted[way][k], EARLY + way * NBR + k, where)
            for c in range(CAP):
                where = jnp.where(named == far + c, LATE + way * CAP + c, where)
            found.append(where)
        place_s[b] = jnp.where(slot < OWN, found[0], jnp.where(slot < 2 * OWN, slot - OWN, found[1]))

    depth = lax.broadcasted_iota(jnp.int32, (LANES, LANES), 0)
    column = lax.broadcasted_iota(jnp.int32, (LANES, LANES), 1)
    band[0] = (jnp.where(depth == column + 1, 0.5, 0.0) - jnp.where(depth == column - 1, 0.5, 0.0)).astype(bf16)
    band[1] = jnp.where(depth == column, 1.0, 0.0).astype(bf16)

    def picked(h, group, c):
        return meta_s[h, 0, CAP * group + c]

    def raw_pair(offset, i, span):
        tile = rows[offset]
        own_span = pl.ds(0, half) if abs(offset) == 3 else span
        own = tile[i, own_span, :]
        up = jnp.where(i == 0, halos[0, offset % G, span, :], tile[jnp.maximum(i - 1, 0), own_span, :]).astype(f32)
        down = jnp.where(
            i == cx - 1, halos[1, offset % G, span, :], tile[jnp.minimum(i + 1, cx - 1), own_span, :]).astype(f32)
        return own, ((down - up) * 0.5).astype(bf16)

    def pass_on(step):
        for way in range(2):
            offset = -(step - 1) if way == 0 else step - 1
            span = raw_half[1 - way] if step == 3 else raw_half[way]
            target = pass3 if step == 3 else pass4
            for c in range(CAP):
                i = picked(at(offset), along(way)[0], c)
                own, grad_x = raw_pair(offset, i, span)
                target[way, c, 0] = own
                target[way, c, 1] = grad_x
            passed(way, step).start()

    def with_border(own, corners, prior, following):
        ends = (jnp.where((depth == following) & (column == LANES - 1), 0.5, 0.0)
                - jnp.where((depth == prior) & (column == 0), 0.5, 0.0)).astype(bf16)
        return jnp.dot(
            jnp.concatenate([own, corners], axis=1), jnp.concatenate([band[0], ends], axis=0),
            preferred_element_type=f32).astype(bf16)

    def keep(offset, pairs, corners):
        h = at(offset)
        for c in range(CAP):
            i = picked(h, me, c)
            own, grad_x = pairs(c, i)
            grad_y = with_border(own, corners, 16 * (h - 1) + 8 + i, 16 * (h + 1) + i)
            whole = jnp.concatenate([own, grad_x, grad_y], axis=1)
            pool[CAP * h + c] = whole
            tiles[CAP * h + c] = whole

    for step in range(1, 5):
        ways = (0, 1) if step < 4 else (0,)
        for way in ways:
            note_copy(way, step, True).wait_recv()
            edge_copy(way, step, True).wait_recv()
            if step < 3 or (step == 3 and way == 0):
                note_copy(way, step + 1).start()
                edge_copy(way, step + 1).start()
            to_smem(-step if way == 0 else step).start()
        if step == 4:
            break
        for c in ORDER:
            for way in range(2):
                ring(way, step, c).wait_recv()
                if step < 3:
                    ring(way, step + 1, c).start()
                offset = -step if way == 0 else step
                if c == 0:
                    send_halo(1, offset)
                if c == 3:
                    send_halo(0, offset)
        if step >= 2:
            for offset in (-step, step):
                halos_arrived(offset)
                to_smem(offset).wait()
            pass_on(step + 1)

    for offset in (0, -1, 1):
        halos_arrived(offset)
        to_smem(offset).wait()
    to_smem(-4).wait()
    everything = pl.ds(0, channels)
    corners = transposed(edges[...].reshape(G * 16, channels), band[1])
    for offset in (0, -1, 1, -2, 2):
        keep(offset, lambda c, i, offset=offset: raw_pair(offset, i, everything), corners)
    for way, offset in ((0, -3), (1, 3)):
        passed(way, 3).wait_recv()

        def pairs(c, i, way=way, offset=offset):
            raw = raw_pair(offset, i, raw_half[way])
            come = (got3[way, c, 0], got3[way, c, 1])
            return tuple(
                jnp.concatenate([a, b] if way == 0 else [b, a], axis=0) for a, b in zip(raw, come))

        keep(offset, pairs, corners)

    def serve(way):
        ask(1 - way).wait_recv()
        to_scalar = pltpu.make_async_copy(asked.at[1 - way], asked_s.at[1 - way], local_sem.at[G + way])
        to_scalar.start()
        to_scalar.wait()
        chosen = jnp.zeros((16, G * 16), f32)
        slots = [asked_s[1 - way, 0, way * NBR + k] for k in range(NBR)] + [far + c for c in range(CAP)]
        for k, slot in enumerate(slots):
            if k < NBR:
                stage[way, k, 0] = pool[slot, :, :LANES]
                stage[way, k, 1] = pool[slot, :, LANES:2 * LANES]
                near_copy(way, k).start()
            h = lax.shift_right_logical(slot, 1)
            i = picked(h, me, slot - 2 * h)
            chosen = jnp.where((line == 2 * k) & (spot == 16 * (h - 1) + 8 + i), 1.0, chosen)
            chosen = jnp.where((line == 2 * k + 1) & (spot == 16 * (h + 1) + i), 1.0, chosen)
        fringe_out[way] = jnp.dot(
            chosen.astype(bf16), edges[...].reshape(G * 16, channels), preferred_element_type=f32).astype(bf16)
        fringe_copy(way).start()

    for way in range(2):
        @pl.when(there[way])
        def _(way=way):
            serve(way)

    for chain in range(2):
        passed(chain, 4).wait_recv()
        for way in range(2):
            @pl.when(there[way])
            def _(way=way):
                late_copy(way, chain).start()
    keep(4, lambda c, i: tuple(jnp.concatenate([got4[0, c, p], got4[1, c, p]], axis=0) for p in range(2)), corners)

    def from_neighbour(way, k, own, grad_x, sides):
        grad_y = with_border(own, sides, 16 * way + 2 * k, 16 * way + 2 * k + 1)
        return jnp.concatenate([own, grad_x, grad_y], axis=1)

    for way in range(2):
        @pl.when(there[1 - way])
        def _(way=way):
            fringe_copy(way).wait_recv()
            for k in range(NBR):
                near_copy(way, k).wait_recv()
    sides = transposed(fringe[...], band[1])
    for way in range(2):
        @pl.when(there[1 - way])
        def _(way=way):
            for k in range(NBR):
                tiles[EARLY + way * NBR + k] = from_neighbour(way, k, near[way, k, 0], near[way, k, 1], sides)
    w_copy.wait()
    for way in range(2):
        @pl.when(there[1 - way])
        def _(way=way):
            for chain in range(2):
                late_copy(way, chain).wait_recv()
            for c in range(CAP):
                own, grad_x = (
                    jnp.concatenate([late[way, 0, c, p], late[way, 1, c, p]], axis=0) for p in range(2))
                tiles[LATE + way * CAP + c] = from_neighbour(way, NBR + c, own, grad_x, sides)

    @pl.loop(0, blocks // 4)
    def _(quarter):
        for k in range(4):
            b = quarter * 4 + k
            part[b] = jnp.dot(tiles[place_s[b]], weights[b], preferred_element_type=f32)

    height = 16

    @pl.loop(0, channels // height)
    def _(strip):
        here = pl.ds(pl.multiple_of(strip * height, height), height)
        sums = [jnp.zeros((height, LANES), f32) for _ in range(OCN)]
        for b in range(blocks):
            value = part[b, here, :]
            for t in range(OCN):
                sums[t] = sums[t] + value * (ocn_ref[b] == t).astype(f32)
        for t in range(OCN):
            out_ref[here, t * LANES:(t + 1) * LANES] = sums[t].astype(bf16)

    for way in range(2):
        for step in range(1, 4):
            for c in ORDER:
                ring(way, step, c).wait_send()
        for step in (3, 4):
            passed(way, step).wait_send()
        for step in range(1, 5 - way):
            note_copy(way, step).wait_send()
            edge_copy(way, step).wait_send()

        @pl.when(there[way])
        def _(way=way):
            ask(way).wait_send()
            for offset in rows:
                halo(way, offset).wait_send()
            for k in range(NBR):
                near_copy(way, k).wait_send()
            fringe_copy(way).wait_send()
            for chain in range(2):
                late_copy(way, chain).wait_send()


def solution(mesh):
    regions = mesh.shape["reg"]

    def per_device(field, send_pick, blk_src, blk_ocn, blk_weight):
        channels, cx, cells = field.shape
        blocks = blk_src.shape[0]
        half = channels // 2
        dma = pltpu.SemaphoreType.DMA
        bf16, f32, i32 = jnp.bfloat16, jnp.float32, jnp.int32
        operands = [
            pltpu.with_memory_space_constraint(x, pltpu.HBM) for x in (field, send_pick, blk_src, blk_ocn, blk_weight)
        ]
        return pl.pallas_call(
            functools.partial(kernel, regions),
            out_shape=jax.ShapeDtypeStruct((channels, OCN * cells), bf16),
            in_specs=[pl.BlockSpec(memory_space=pl.ANY)] * 5,
            out_specs=pl.BlockSpec(memory_space=pltpu.VMEM),
            scratch_shapes=[
                pltpu.VMEM(field.shape, bf16),
                pltpu.SMEM(send_pick.shape, i32),
                pltpu.SMEM(blk_src.shape, i32),
                pltpu.SMEM(blk_ocn.shape, i32),
                pltpu.VMEM((cx, channels, cells), bf16),
                pltpu.VMEM((cx, channels, cells), bf16),
                pltpu.VMEM((cx, channels, cells), bf16),
                pltpu.VMEM((cx, half, cells), bf16),
                pltpu.VMEM((cx, half, cells), bf16),
                pltpu.VMEM((cx, channels, cells), bf16),
                pltpu.VMEM((cx, channels, cells), bf16),
                pltpu.VMEM((2, G, channels, cells), bf16),
                pltpu.VMEM((G, 16, channels), bf16),
                pltpu.VMEM((8, LANES), i32),
                pltpu.VMEM((LANES, channels), bf16),
                pltpu.VMEM((2, CAP, 2, half, cells), bf16),
                pltpu.VMEM((2, CAP, 2, half, cells), bf16),
                pltpu.VMEM((2, CAP, 2, half, cells), bf16),
                pltpu.VMEM((2, CAP, 2, half, cells), bf16),
                pltpu.VMEM((OWN, channels, 3 * cells), bf16),
                pltpu.VMEM((SLOTS, channels, 3 * cells), bf16),
                pltpu.VMEM((2, NBR, 2, channels, cells), bf16),
                pltpu.VMEM((2, NBR, 2, channels, cells), bf16),
                pltpu.VMEM((2, 2, CAP, 2, half, cells), bf16),
                pltpu.VMEM((blocks, 3 * cells, cells), bf16),
                pltpu.VMEM((channels * cx, cells), f32),
                pltpu.VMEM((G, 8, LANES), i32),
                pltpu.VMEM((2, 8, LANES), i32),
                pltpu.SMEM((G, 8, LANES), i32),
                pltpu.SMEM((2, 8, LANES), i32),
                pltpu.SMEM((blocks,), i32),
                pltpu.VMEM((2, LANES, LANES), bf16),
                pltpu.VMEM((blocks, channels, cells), f32),
                pltpu.VMEM((2, 16, channels), bf16),
                dma((2, 3, 4)), dma((2, 3, 4)),
                dma((2, 2)), dma((2, 2)),
                dma((2, 4)), dma((2, 4)),
                dma((2, 4)), dma((2, 4)),
                dma((2, G)), dma((2, G)),
                dma((2,)), dma((2,)),
                dma((2, NBR)), dma((2, NBR)),
                dma((2,)), dma((2,)),
                dma((2, 2)), dma((2, 2)),
                dma((G + 2,)),
                dma((4,)),
                dma,
            ],
            compiler_params=pltpu.CompilerParams(
                collective_id=0, has_side_effects=True, vmem_limit_bytes=VMEM_LIMIT
            ),
            cost_estimate=pl.CostEstimate(
                flops=2 * blocks * channels * 3 * cells * cells, bytes_accessed=4 * 1024 * 1024, transcendentals=0
            ),
        )(*operands)

    placed = (
        P(None, "reg", "grp"),
        P(("grp", "reg")),
        P(("grp", "reg")),
        P(("grp", "reg")),
        P(("grp", "reg"), None, None),
    )
    return jax.shard_map(
        per_device, mesh=mesh, in_specs=placed, out_specs=P(None, ("grp", "reg")), check_vma=False
    )
```

```python
import functools

import jax
import jax.numpy as jnp
from jax import lax
from jax.experimental import pallas as pl
from jax.experimental.pallas import tpu as pltpu
from jax.sharding import PartitionSpec as P

MESH = pl.DeviceIdType.MESH
OCN = 4
CAP = 2
NBR = 4
G = 8
LANES = 128
VMEM_LIMIT = 48 * 1024 * 1024
ORDER = (0, 3, 1, 2)
OWN = G * CAP
EARLY, LATE = OWN, OWN + 2 * NBR
LAST = (-3, 3, 4)
SLOTS = LATE + 2 * CAP * len(LAST)


def transposed(matrix, unit):
    return lax.dot_general(
        unit, matrix, (((1,), (1,)), ((), ())), preferred_element_type=jnp.float32
    ).astype(jnp.bfloat16)


def distinct(src_ref, low):
    found = [jnp.int32(0)] * NBR
    count = jnp.int32(0)
    for b in range(src_ref.shape[0]):
        slot = src_ref[b] - low
        fresh = (slot >= 0) & (slot < OWN)
        for k in range(NBR):
            fresh = fresh & ((count <= k) | (found[k] != slot))
        for k in range(NBR):
            found[k] = jnp.where(fresh & (count == k), slot, found[k])
        count = count + fresh.astype(jnp.int32)
    return found


def kernel(regions, field_hbm, pick_hbm, src_hbm, ocn_hbm, w_hbm, out_ref,
           field_ref, pick_ref, src_ref, ocn_ref,
           row0, row1, row2, row3, row5, row6, row7, halos, edges, wish, fringe,
           pass3, pass4, got3, got4, raw3, pairs, tiles, stage, near, late, weights, flat,
           meta, asked, meta_s, asked_s, place_s, band, part_a, part_b, sums, fringe_out,
           ring_send, ring_recv, pass_send, pass_recv, meta_send, meta_recv, edge_send, edge_recv,
           halo_send, halo_recv, ask_send, ask_recv, near_send, near_recv, fringe_send, fringe_recv,
           late_send, late_recv, local_sem, in_sem, w_sem):
    me = lax.axis_index("grp")
    r = lax.axis_index("reg")
    rows = {0: row0, 1: row1, 2: row2, 3: row3, -3: row5, -2: row6, -1: row7}
    channels, cx = field_ref.shape[:2]
    half = channels // 2
    first, second = pl.ds(0, half), pl.ds(half, half)
    raw_half = (first, second)
    blocks = src_ref.shape[0]
    f32, bf16 = jnp.float32, jnp.bfloat16
    right, left = lax.rem(me + 1, G), lax.rem(me + G - 1, G)
    has_low, has_high = r > 0, r < regions - 1
    low, high = jnp.maximum(r - 1, 0), jnp.minimum(r + 1, regions - 1)
    there = (has_high, has_low)

    def at(offset):
        return lax.rem(me + offset + G, G)

    def along(way):
        return (right if way == 0 else left, r)

    def across(way):
        return (me, high if way == 0 else low)

    def remote(source, target, send, receive, device):
        return pltpu.make_async_remote_copy(
            src_ref=source, dst_ref=target, send_sem=send, recv_sem=receive, device_id=device, device_id_type=MESH)

    arriving = [
        pltpu.make_async_copy(origin, here, in_sem.at[k])
        for k, (origin, here) in enumerate(
            ((field_hbm, field_ref), (pick_hbm, pick_ref), (src_hbm, src_ref), (ocn_hbm, ocn_ref)))
    ]
    for copy in arriving:
        copy.start()
    barrier = pltpu.get_barrier_semaphore()
    for way in range(2):
        pl.semaphore_signal(barrier, inc=1, device_id=along(way), device_id_type=MESH)

    for way in range(2):
        @pl.when(there[way])
        def _(way=way):
            pl.semaphore_signal(barrier, inc=1, device_id=across(way), device_id_type=MESH)

    w_copy = pltpu.make_async_copy(w_hbm, weights, w_sem)
    w_copy.start()

    fringe[...] = jnp.zeros(fringe.shape, bf16)
    for offset in LAST:
        for c in range(CAP):
            pairs[CAP * at(offset) + c] = jnp.zeros(pairs.shape[1:], bf16)

    for way in range(2):
        @pl.when(jnp.logical_not(there[1 - way]))
        def _(way=way):
            for d in range(G):
                halos[way, d] = jnp.zeros(halos.shape[2:], bf16)
            for k in range(NBR):
                tiles[EARLY + way * NBR + k] = jnp.zeros(tiles.shape[1:], bf16)
            for k in range(CAP * len(LAST)):
                tiles[LATE + way * CAP * len(LAST) + k] = jnp.zeros(tiles.shape[1:], bf16)

    arriving[0].wait()
    flat[...] = field_ref[...].astype(f32).reshape(flat.shape)
    for i in range(cx):
        row0[i] = flat[pl.ds(i, channels, stride=cx), :].astype(bf16)

    pl.semaphore_wait(barrier, 2 + has_low.astype(jnp.int32) + has_high.astype(jnp.int32))

    def ring(way, step, c):
        sign = -1 if way == 0 else 1
        source = rows[sign * (step - 1)].at[pl.ds(2 * c, 2)]
        if step == 3:
            source = rows[sign * 2].at[pl.ds(2 * c, 2), raw_half[way]]
        return remote(source, rows[sign * step].at[pl.ds(2 * c, 2)],
                      ring_send.at[way, step - 1, c], ring_recv.at[way, step - 1, c], along(way))

    def passed(way, step):
        source, target = (pass3, got3) if step == 3 else (pass4, got4)
        return remote(source.at[way], target.at[way],
                      pass_send.at[way, step - 3], pass_recv.at[way, step - 3], along(way))

    def note_copy(way, step, receiving=False):
        sign = -1 if way == 0 else 1
        h = at(sign * (step if receiving else step - 1))
        return remote(meta.at[h], meta.at[h], meta_send.at[way, step - 1], meta_recv.at[way, step - 1], along(way))

    def edge_copy(way, step, receiving=False):
        sign = -1 if way == 0 else 1
        h = at(sign * (step if receiving else step - 1))
        return remote(edges.at[h], edges.at[h], edge_send.at[way, step - 1], edge_recv.at[way, step - 1], along(way))

    def to_smem(offset):
        h = at(offset)
        return pltpu.make_async_copy(meta.at[h], meta_s.at[h], local_sem.at[offset % G])

    def halo(way, offset):
        source = rows[offset].at[cx - 1 if way == 0 else 0]
        target = halos.at[way, offset % G]
        if abs(offset) == 3:
            target = halos.at[way, offset % G, first if offset < 0 else second]
        return remote(source, target, halo_send.at[way, offset % G], halo_recv.at[way, offset % G], across(way))

    def send_halo(way, offset):
        @pl.when(there[way])
        def _():
            halo(way, offset).start()

    def halos_arrived(offset):
        for way in range(2):
            @pl.when(there[1 - way])
            def _(way=way):
                halo(way, offset).wait_recv()

    def ask(way):
        return remote(wish, asked.at[way], ask_send.at[way], ask_recv.at[way], across(way))

    def near_copy(way, k):
        return remote(stage.at[way, k], near.at[way, k], near_send.at[way, k], near_recv.at[way, k], across(way))

    def fringe_copy(way):
        return remote(fringe_out.at[way], fringe.at[pl.ds(32 * way, 32)],
                      fringe_send.at[way], fringe_recv.at[way], across(way))

    def late_copy(way, kind, chain):
        return remote((raw3, got3, got4)[kind].at[chain], late.at[way, kind, chain],
                      late_send.at[way, kind, chain], late_recv.at[way, kind, chain], across(way))

    def send_late(kind, chain):
        for way in range(2):
            @pl.when(there[way])
            def _(way=way):
                late_copy(way, kind, chain).start()

    for c in ORDER:
        for way in range(2):
            ring(way, 1, c).start()
        if c == 3:
            for way in range(2):
                send_halo(way, 0)

    for copy in arriving[1:]:
        copy.wait()
    lane = lax.broadcasted_iota(jnp.int32, (8, LANES), 1)
    note = jnp.zeros((8, LANES), jnp.int32)
    for k in range(OWN):
        note = jnp.where(lane == k, pick_ref[k], note)
    meta[me] = note
    line = lax.broadcasted_iota(jnp.int32, (16, LANES), 0)
    spot = lax.broadcasted_iota(jnp.int32, (16, LANES), 1)
    border = jnp.zeros((16, channels), f32)
    for i in range(cx):
        chosen = ((line == i) & (spot == 0)) | ((line == 8 + i) & (spot == LANES - 1))
        border = border + lax.dot_general(
            jnp.where(chosen, 1.0, 0.0).astype(bf16), row0[i], (((1,), (1,)), ((), ())), preferred_element_type=f32)
    edges[me] = border.astype(bf16)
    for way in range(2):
        note_copy(way, 1).start()
        edge_copy(way, 1).start()
    to_smem(0).start()

    wanted = (distinct(src_ref, 0), distinct(src_ref, 2 * OWN))
    request = jnp.zeros((8, LANES), jnp.int32)
    for way in range(2):
        for k in range(NBR):
            request = jnp.where(lane == way * NBR + k, wanted[way][k], request)
    wish[...] = request
    for way in range(2):
        @pl.when(there[way])
        def _(way=way):
            ask(way).start()
    far = [CAP * at(offset) + c for offset in LAST for c in range(CAP)]
    for b in range(blocks):
        slot = src_ref[b]
        found = []
        for way in range(2):
            named = slot - 2 * OWN * way
            where = jnp.int32(EARLY + way * NBR)
            for k in range(1, NBR):
                where = jnp.where(named == wanted[way][k], EARLY + way * NBR + k, where)
            for k, slot_of in enumerate(far):
                where = jnp.where(named == slot_of, LATE + way * len(far) + k, where)
            found.append(where)
        place_s[b] = jnp.where(slot < OWN, found[0], jnp.where(slot < 2 * OWN, slot - OWN, found[1]))

    depth = lax.broadcasted_iota(jnp.int32, (LANES, LANES), 0)
    column = lax.broadcasted_iota(jnp.int32, (LANES, LANES), 1)
    band[0] = (jnp.where(depth == column + 1, 0.5, 0.0) - jnp.where(depth == column - 1, 0.5, 0.0)).astype(bf16)
    band[1] = jnp.where(depth == column, 1.0, 0.0).astype(bf16)

    def picked(h, group, c):
        return meta_s[h, 0, CAP * group + c]

    def raw_pair(offset, i, span):
        tile = rows[offset]
        own_span = pl.ds(0, half) if abs(offset) == 3 else span
        own = tile[i, own_span, :]
        up = jnp.where(i == 0, halos[0, offset % G, span, :], tile[jnp.maximum(i - 1, 0), own_span, :]).astype(f32)
        down = jnp.where(
            i == cx - 1, halos[1, offset % G, span, :], tile[jnp.minimum(i + 1, cx - 1), own_span, :]).astype(f32)
        return own, ((down - up) * 0.5).astype(bf16)

    def pass_on(step):
        for way in range(2):
            offset = -(step - 1) if way == 0 else step - 1
            span = raw_half[1 - way] if step == 3 else raw_half[way]
            target = pass3 if step == 3 else pass4
            for c in range(CAP):
                i = picked(at(offset), along(way)[0], c)
                own, grad_x = raw_pair(offset, i, span)
                target[way, c, 0] = own
                target[way, c, 1] = grad_x
            passed(way, step).start()

    def with_border(own, corners, prior, following):
        ends = (jnp.where((depth == following) & (column == LANES - 1), 0.5, 0.0)
                - jnp.where((depth == prior) & (column == 0), 0.5, 0.0)).astype(bf16)
        return jnp.dot(
            jnp.concatenate([own, corners], axis=1), jnp.concatenate([band[0], ends], axis=0),
            preferred_element_type=f32).astype(bf16)

    def joined(a, b):
        return jnp.concatenate([a, b], axis=0)

    def keep(offset, pair, corners):
        h = at(offset)
        for c in range(CAP):
            i = picked(h, me, c)
            own, grad_x = pair(h, c)
            grad_y = with_border(own, corners, 16 * (h - 1) + 8 + i, 16 * (h + 1) + i)
            whole = jnp.concatenate([own, grad_x, grad_y], axis=1)
            tiles[CAP * h + c] = whole

    def serve(way):
        ask(1 - way).wait_recv()
        to_scalar = pltpu.make_async_copy(asked.at[1 - way], asked_s.at[1 - way], local_sem.at[G + way])
        to_scalar.start()
        to_scalar.wait()
        for k in range(NBR):
            stage[way, k] = pairs[asked_s[1 - way, 0, way * NBR + k]]
            near_copy(way, k).start()

    def send_fringe(way):
        row = lax.broadcasted_iota(jnp.int32, (32, LANES), 0)
        place = lax.broadcasted_iota(jnp.int32, (32, LANES), 1)
        chosen = jnp.zeros((32, LANES), f32)
        for k, slot in enumerate([asked_s[1 - way, 0, way * NBR + k] for k in range(NBR)] + far):
            h = lax.shift_right_logical(slot, 1)
            i = picked(h, me, slot - 2 * h)
            chosen = jnp.where((row == 2 * k) & (place == 16 * (h - 1) + 8 + i), 1.0, chosen)
            chosen = jnp.where((row == 2 * k + 1) & (place == 16 * (h + 1) + i), 1.0, chosen)
        fringe_out[way] = jnp.dot(
            chosen.astype(bf16), edges[...].reshape(G * 16, channels), preferred_element_type=f32).astype(bf16)
        fringe_copy(way).start()

    everything = pl.ds(0, channels)
    for step in range(1, 5):
        ways = (0, 1) if step < 4 else (0,)
        for way in ways:
            note_copy(way, step, True).wait_recv()
            edge_copy(way, step, True).wait_recv()
            if step < 3 or (step == 3 and way == 0):
                note_copy(way, step + 1).start()
                edge_copy(way, step + 1).start()
            to_smem(-step if way == 0 else step).start()
        if step == 4:
            break
        for c in ORDER:
            for way in range(2):
                ring(way, step, c).wait_recv()
                if step < 3:
                    ring(way, step + 1, c).start()
                offset = -step if way == 0 else step
                if c == 0:
                    send_halo(1, offset)
                if c == 3:
                    send_halo(0, offset)
        if step >= 2:
            for offset in (-step, step):
                halos_arrived(offset)
                to_smem(offset).wait()
            pass_on(step + 1)
        if step == 2:
            for offset in (0, -1, 1):
                halos_arrived(offset)
                to_smem(offset).wait()
            for offset in (0, -1, 1, -2, 2):
                for c in range(CAP):
                    h = at(offset)
                    own, grad_x = raw_pair(offset, picked(h, me, c), everything)
                    pairs[CAP * h + c, 0] = own
                    pairs[CAP * h + c, 1] = grad_x
            for way in range(2):
                @pl.when(there[way])
                def _(way=way):
                    serve(way)
        if step == 3:
            for way, offset in ((0, -3), (1, 3)):
                for c in range(CAP):
                    own, grad_x = raw_pair(offset, picked(at(offset), me, c), raw_half[way])
                    raw3[way, c, 0] = own
                    raw3[way, c, 1] = grad_x
                send_late(0, way)

    to_smem(-4).wait()
    for chain in range(2):
        passed(chain, 3).wait_recv()
        send_late(1, chain)
    for way in range(2):
        @pl.when(there[way])
        def _(way=way):
            send_fringe(way)
    corners = transposed(edges[...].reshape(G * 16, channels), band[1])
    for offset in (0, -1, 1, -2, 2):
        keep(offset, lambda h, c: (pairs[CAP * h + c, 0], pairs[CAP * h + c, 1]), corners)
    keep(-3, lambda h, c: tuple(joined(raw3[0, c, p], got3[0, c, p]) for p in range(2)), corners)
    keep(3, lambda h, c: tuple(joined(got3[1, c, p], raw3[1, c, p]) for p in range(2)), corners)
    for chain in range(2):
        passed(chain, 4).wait_recv()
        send_late(2, chain)
    keep(4, lambda h, c: tuple(joined(got4[0, c, p], got4[1, c, p]) for p in range(2)), corners)

    def from_neighbour(way, k, own, grad_x, sides):
        grad_y = with_border(own, sides, 32 * way + 2 * k, 32 * way + 2 * k + 1)
        return jnp.concatenate([own, grad_x, grad_y], axis=1)

    for way in range(2):
        @pl.when(there[1 - way])
        def _(way=way):
            fringe_copy(way).wait_recv()
            for k in range(NBR):
                near_copy(way, k).wait_recv()
    sides = transposed(fringe[...], band[1])
    for way in range(2):
        @pl.when(there[1 - way])
        def _(way=way):
            for k in range(NBR):
                tiles[EARLY + way * NBR + k] = from_neighbour(way, k, near[way, k, 0], near[way, k, 1], sides)
    w_copy.wait()

    def late_tile(way, offset, c):
        halves = {-3: ((0, 0), (1, 0)), 3: ((1, 1), (0, 1)), 4: ((2, 0), (2, 1))}[offset]
        own, grad_x = (joined(*[late[way, kind, chain, c, p] for kind, chain in halves]) for p in range(2))
        k = CAP * LAST.index(offset) + c
        tiles[LATE + way * len(far) + k] = from_neighbour(way, NBR + k, own, grad_x, sides)

    for kinds, offsets in (((0, 1), (-3, 3)), ((2,), (4,))):
        for way in range(2):
            @pl.when(there[1 - way])
            def _(way=way):
                for kind in kinds:
                    for chain in range(2):
                        late_copy(way, kind, chain).wait_recv()
                for offset in offsets:
                    for c in range(CAP):
                        late_tile(way, offset, c)

    def multiply(part, start):
        for k in range(4):
            part[k] = jnp.dot(tiles[place_s[start + k]], weights[start + k], preferred_element_type=f32)

    def add(part, start, live):
        mine = [[((ocn_ref[start + k] == t) & live).astype(f32) for k in range(4)] for t in range(OCN)]
        for strip in range(channels // 16):
            here = pl.ds(16 * strip, 16)
            values = [part[k, here, :] for k in range(4)]
            for t in range(OCN):
                total = sums[t, here, :]
                for k in range(4):
                    total = total + values[k] * mine[t][k]
                sums[t, here, :] = total

    part_b[...] = jnp.zeros(part_b.shape, f32)
    sums[...] = jnp.zeros(sums.shape, f32)

    @pl.loop(0, blocks // 8)
    def _(eight):
        start = eight * 8
        multiply(part_a, start)
        add(part_b, jnp.maximum(start - 4, 0), eight > 0)
        multiply(part_b, start + 4)
        add(part_a, start, True)

    add(part_b, blocks - 4, True)
    for t in range(OCN):
        out_ref[:, t * LANES:(t + 1) * LANES] = sums[t].astype(bf16)

    for way in range(2):
        for step in range(1, 4):
            for c in ORDER:
                ring(way, step, c).wait_send()
        for step in (3, 4):
            passed(way, step).wait_send()
        for step in range(1, 5 - way):
            note_copy(way, step).wait_send()
            edge_copy(way, step).wait_send()

        @pl.when(there[way])
        def _(way=way):
            ask(way).wait_send()
            for offset in rows:
                halo(way, offset).wait_send()
            for k in range(NBR):
                near_copy(way, k).wait_send()
            fringe_copy(way).wait_send()
            for kind in range(3):
                for chain in range(2):
                    late_copy(way, kind, chain).wait_send()


def solution(mesh):
    regions = mesh.shape["reg"]

    def per_device(field, send_pick, blk_src, blk_ocn, blk_weight):
        channels, cx, cells = field.shape
        blocks = blk_src.shape[0]
        half = channels // 2
        dma = pltpu.SemaphoreType.DMA
        bf16, f32, i32 = jnp.bfloat16, jnp.float32, jnp.int32
        operands = [
            pltpu.with_memory_space_constraint(x, pltpu.HBM) for x in (field, send_pick, blk_src, blk_ocn, blk_weight)
        ]
        return pl.pallas_call(
            functools.partial(kernel, regions),
            out_shape=jax.ShapeDtypeStruct((channels, OCN * cells), bf16),
            in_specs=[pl.BlockSpec(memory_space=pl.ANY)] * 5,
            out_specs=pl.BlockSpec(memory_space=pltpu.VMEM),
            scratch_shapes=[
                pltpu.VMEM(field.shape, bf16),
                pltpu.SMEM(send_pick.shape, i32),
                pltpu.SMEM(blk_src.shape, i32),
                pltpu.SMEM(blk_ocn.shape, i32),
                pltpu.VMEM((cx, channels, cells), bf16),
                pltpu.VMEM((cx, channels, cells), bf16),
                pltpu.VMEM((cx, channels, cells), bf16),
                pltpu.VMEM((cx, half, cells), bf16),
                pltpu.VMEM((cx, half, cells), bf16),
                pltpu.VMEM((cx, channels, cells), bf16),
                pltpu.VMEM((cx, channels, cells), bf16),
                pltpu.VMEM((2, G, channels, cells), bf16),
                pltpu.VMEM((G, 16, channels), bf16),
                pltpu.VMEM((8, LANES), i32),
                pltpu.VMEM((LANES, channels), bf16),
                pltpu.VMEM((2, CAP, 2, half, cells), bf16),
                pltpu.VMEM((2, CAP, 2, half, cells), bf16),
                pltpu.VMEM((2, CAP, 2, half, cells), bf16),
                pltpu.VMEM((2, CAP, 2, half, cells), bf16),
                pltpu.VMEM((2, CAP, 2, half, cells), bf16),
                pltpu.VMEM((OWN, 2, channels, cells), bf16),
                pltpu.VMEM((SLOTS, channels, 3 * cells), bf16),
                pltpu.VMEM((2, NBR, 2, channels, cells), bf16),
                pltpu.VMEM((2, NBR, 2, channels, cells), bf16),
                pltpu.VMEM((2, 3, 2, CAP, 2, half, cells), bf16),
                pltpu.VMEM((blocks, 3 * cells, cells), bf16),
                pltpu.VMEM((channels * cx, cells), f32),
                pltpu.VMEM((G, 8, LANES), i32),
                pltpu.VMEM((2, 8, LANES), i32),
                pltpu.SMEM((G, 8, LANES), i32),
                pltpu.SMEM((2, 8, LANES), i32),
                pltpu.SMEM((blocks,), i32),
                pltpu.VMEM((2, LANES, LANES), bf16),
                pltpu.VMEM((4, channels, cells), f32),
                pltpu.VMEM((4, channels, cells), f32),
                pltpu.VMEM((OCN, channels, cells), f32),
                pltpu.VMEM((2, 32, channels), bf16),
                dma((2, 3, 4)), dma((2, 3, 4)),
                dma((2, 2)), dma((2, 2)),
                dma((2, 4)), dma((2, 4)),
                dma((2, 4)), dma((2, 4)),
                dma((2, G)), dma((2, G)),
                dma((2,)), dma((2,)),
                dma((2, NBR)), dma((2, NBR)),
                dma((2,)), dma((2,)),
                dma((2, 3, 2)), dma((2, 3, 2)),
                dma((G + 2,)),
                dma((4,)),
                dma,
            ],
            compiler_params=pltpu.CompilerParams(
                collective_id=0, has_side_effects=True, vmem_limit_bytes=VMEM_LIMIT
            ),
            cost_estimate=pl.CostEstimate(
                flops=2 * blocks * channels * 3 * cells * cells, bytes_accessed=4 * 1024 * 1024, transcendentals=0
            ),
        )(*operands)

    placed = (
        P(None, "reg", "grp"),
        P(("grp", "reg")),
        P(("grp", "reg")),
        P(("grp", "reg")),
        P(("grp", "reg"), None, None),
    )
    return jax.shard_map(
        per_device, mesh=mesh, in_specs=placed, out_specs=P(None, ("grp", "reg")), check_vma=False
    )
```

```python
import functools

import jax
import jax.numpy as jnp
from jax import lax
from jax.experimental import pallas as pl
from jax.experimental.pallas import tpu as pltpu
from jax.sharding import PartitionSpec as P

MESH = pl.DeviceIdType.MESH
OCN = 4
CAP = 2
NBR = 4
G = 8
LANES = 128
VMEM_LIMIT = 48 * 1024 * 1024
ORDER = (0, 7, 1, 2, 3, 4, 5, 6)
DEPTH = 5
OWN = G * CAP
EARLY, LATE = OWN, OWN + 2 * NBR
LAST = (-3, 3, 4)
SLOTS = LATE + 2 * CAP * len(LAST)


def transposed(matrix, unit):
    return lax.dot_general(
        unit, matrix, (((1,), (1,)), ((), ())), preferred_element_type=jnp.float32
    ).astype(jnp.bfloat16)


def distinct(src_ref, low):
    found = [jnp.int32(0)] * NBR
    count = jnp.int32(0)
    for b in range(src_ref.shape[0]):
        slot = src_ref[b] - low
        fresh = (slot >= 0) & (slot < OWN)
        for k in range(NBR):
            fresh = fresh & ((count <= k) | (found[k] != slot))
        for k in range(NBR):
            found[k] = jnp.where(fresh & (count == k), slot, found[k])
        count = count + fresh.astype(jnp.int32)
    return found


def kernel(regions, field_hbm, pick_hbm, src_hbm, ocn_hbm, w_hbm, out_ref,
           field_ref, pick_ref, src_ref, ocn_ref,
           row0, row1, row2, row3, row5, row6, row7, halos, edges, wish, fringe,
           pass3, pass4, got3, got4, raw3, pairs, tiles, stage, near, late, weights, flat,
           meta, asked, meta_s, asked_s, place_s, band, part_a, part_b, sums, fringe_out,
           ring_send, ring_recv, pass_send, pass_recv, meta_send, meta_recv, edge_send, edge_recv,
           halo_send, halo_recv, ask_send, ask_recv, near_send, near_recv, fringe_send, fringe_recv,
           late_send, late_recv, local_sem, in_sem, w_sem):
    me = lax.axis_index("grp")
    r = lax.axis_index("reg")
    rows = {0: row0, 1: row1, 2: row2, 3: row3, -3: row5, -2: row6, -1: row7}
    channels, cx = field_ref.shape[:2]
    half = channels // 2
    first, second = pl.ds(0, half), pl.ds(half, half)
    raw_half = (first, second)
    blocks = src_ref.shape[0]
    f32, bf16 = jnp.float32, jnp.bfloat16
    right, left = lax.rem(me + 1, G), lax.rem(me + G - 1, G)
    has_low, has_high = r > 0, r < regions - 1
    low, high = jnp.maximum(r - 1, 0), jnp.minimum(r + 1, regions - 1)
    there = (has_high, has_low)

    def at(offset):
        return lax.rem(me + offset + G, G)

    def along(way):
        return (right if way == 0 else left, r)

    def across(way):
        return (me, high if way == 0 else low)

    def remote(source, target, send, receive, device):
        return pltpu.make_async_remote_copy(
            src_ref=source, dst_ref=target, send_sem=send, recv_sem=receive, device_id=device, device_id_type=MESH)

    arriving = [
        pltpu.make_async_copy(origin, here, in_sem.at[k])
        for k, (origin, here) in enumerate(
            ((field_hbm, field_ref), (pick_hbm, pick_ref), (src_hbm, src_ref), (ocn_hbm, ocn_ref)))
    ]
    for copy in arriving:
        copy.start()
    barrier = pltpu.get_barrier_semaphore()
    for way in range(2):
        pl.semaphore_signal(barrier, inc=1, device_id=along(way), device_id_type=MESH)

    for way in range(2):
        @pl.when(there[way])
        def _(way=way):
            pl.semaphore_signal(barrier, inc=1, device_id=across(way), device_id_type=MESH)

    w_copy = pltpu.make_async_copy(w_hbm, weights, w_sem)
    w_copy.start()

    fringe[...] = jnp.zeros(fringe.shape, bf16)
    for offset in LAST:
        for c in range(CAP):
            pairs[CAP * at(offset) + c] = jnp.zeros(pairs.shape[1:], bf16)

    for way in range(2):
        @pl.when(jnp.logical_not(there[1 - way]))
        def _(way=way):
            for d in range(G):
                halos[way, d] = jnp.zeros(halos.shape[2:], bf16)
            for k in range(NBR):
                tiles[EARLY + way * NBR + k] = jnp.zeros(tiles.shape[1:], bf16)
            for k in range(CAP * len(LAST)):
                tiles[LATE + way * CAP * len(LAST) + k] = jnp.zeros(tiles.shape[1:], bf16)

    arriving[0].wait()
    flat[...] = field_ref[...].astype(f32).reshape(flat.shape)
    for i in range(cx):
        row0[i] = flat[pl.ds(i, channels, stride=cx), :].astype(bf16)

    pl.semaphore_wait(barrier, 2 + has_low.astype(jnp.int32) + has_high.astype(jnp.int32))

    def ring(way, step, c):
        sign = -1 if way == 0 else 1
        source = rows[sign * (step - 1)].at[pl.ds(c, 1)]
        if step == 3:
            source = rows[sign * 2].at[pl.ds(c, 1), raw_half[way]]
        return remote(source, rows[sign * step].at[pl.ds(c, 1)],
                      ring_send.at[way, step - 1, c], ring_recv.at[way, step - 1, c], along(way))

    def passed(way, step):
        source, target = (pass3, got3) if step == 3 else (pass4, got4)
        return remote(source.at[way], target.at[way],
                      pass_send.at[way, step - 3], pass_recv.at[way, step - 3], along(way))

    def note_copy(way, step, receiving=False):
        sign = -1 if way == 0 else 1
        h = at(sign * (step if receiving else step - 1))
        return remote(meta.at[h], meta.at[h], meta_send.at[way, step - 1], meta_recv.at[way, step - 1], along(way))

    def edge_copy(way, step, receiving=False):
        sign = -1 if way == 0 else 1
        h = at(sign * (step if receiving else step - 1))
        return remote(edges.at[h], edges.at[h], edge_send.at[way, step - 1], edge_recv.at[way, step - 1], along(way))

    def to_smem(offset):
        h = at(offset)
        return pltpu.make_async_copy(meta.at[h], meta_s.at[h], local_sem.at[offset % G])

    def halo(way, offset):
        source = rows[offset].at[cx - 1 if way == 0 else 0]
        target = halos.at[way, offset % G]
        if abs(offset) == 3:
            target = halos.at[way, offset % G, first if offset < 0 else second]
        return remote(source, target, halo_send.at[way, offset % G], halo_recv.at[way, offset % G], across(way))

    def send_halo(way, offset):
        @pl.when(there[way])
        def _():
            halo(way, offset).start()

    def halos_arrived(offset):
        for way in range(2):
            @pl.when(there[1 - way])
            def _(way=way):
                halo(way, offset).wait_recv()

    def ask(way):
        return remote(wish, asked.at[way], ask_send.at[way], ask_recv.at[way], across(way))

    def near_copy(way, k):
        return remote(stage.at[way, k], near.at[way, k], near_send.at[way, k], near_recv.at[way, k], across(way))

    def fringe_copy(way):
        return remote(fringe_out.at[way], fringe.at[pl.ds(32 * way, 32)],
                      fringe_send.at[way], fringe_recv.at[way], across(way))

    def late_copy(way, kind, chain):
        return remote((raw3, got3, got4)[kind].at[chain], late.at[way, kind, chain],
                      late_send.at[way, kind, chain], late_recv.at[way, kind, chain], across(way))

    def send_late(kind, chain):
        for way in range(2):
            @pl.when(there[way])
            def _(way=way):
                late_copy(way, kind, chain).start()

    under_way = ([], [])

    def send(way, copy):
        if len(under_way[way]) == DEPTH:
            under_way[way].pop(0).wait_send()
        copy.start()
        under_way[way].append(copy)

    for way in range(2):
        send_halo(way, 0)
    for c in ORDER[:DEPTH]:
        for way in range(2):
            send(way, ring(way, 1, c))

    for copy in arriving[1:]:
        copy.wait()
    lane = lax.broadcasted_iota(jnp.int32, (8, LANES), 1)
    note = jnp.zeros((8, LANES), jnp.int32)
    for k in range(OWN):
        note = jnp.where(lane == k, pick_ref[k], note)
    meta[me] = note
    line = lax.broadcasted_iota(jnp.int32, (16, LANES), 0)
    spot = lax.broadcasted_iota(jnp.int32, (16, LANES), 1)
    border = jnp.zeros((16, channels), f32)
    for i in range(cx):
        chosen = ((line == i) & (spot == 0)) | ((line == 8 + i) & (spot == LANES - 1))
        border = border + lax.dot_general(
            jnp.where(chosen, 1.0, 0.0).astype(bf16), row0[i], (((1,), (1,)), ((), ())), preferred_element_type=f32)
    edges[me] = border.astype(bf16)
    for way in range(2):
        note_copy(way, 1).start()
        edge_copy(way, 1).start()
    to_smem(0).start()
    for c in ORDER[DEPTH:]:
        for way in range(2):
            send(way, ring(way, 1, c))

    wanted = (distinct(src_ref, 0), distinct(src_ref, 2 * OWN))
    request = jnp.zeros((8, LANES), jnp.int32)
    for way in range(2):
        for k in range(NBR):
            request = jnp.where(lane == way * NBR + k, wanted[way][k], request)
    wish[...] = request
    for way in range(2):
        @pl.when(there[way])
        def _(way=way):
            ask(way).start()
    far = [CAP * at(offset) + c for offset in LAST for c in range(CAP)]
    for b in range(blocks):
        slot = src_ref[b]
        found = []
        for way in range(2):
            named = slot - 2 * OWN * way
            where = jnp.int32(EARLY + way * NBR)
            for k in range(1, NBR):
                where = jnp.where(named == wanted[way][k], EARLY + way * NBR + k, where)
            for k, slot_of in enumerate(far):
                where = jnp.where(named == slot_of, LATE + way * len(far) + k, where)
            found.append(where)
        place_s[b] = jnp.where(slot < OWN, found[0], jnp.where(slot < 2 * OWN, slot - OWN, found[1]))

    depth = lax.broadcasted_iota(jnp.int32, (LANES, LANES), 0)
    column = lax.broadcasted_iota(jnp.int32, (LANES, LANES), 1)
    band[0] = (jnp.where(depth == column + 1, 0.5, 0.0) - jnp.where(depth == column - 1, 0.5, 0.0)).astype(bf16)
    band[1] = jnp.where(depth == column, 1.0, 0.0).astype(bf16)

    def picked(h, group, c):
        return meta_s[h, 0, CAP * group + c]

    def raw_pair(offset, i, span):
        tile = rows[offset]
        own_span = pl.ds(0, half) if abs(offset) == 3 else span
        own = tile[i, own_span, :]
        up = jnp.where(i == 0, halos[0, offset % G, span, :], tile[jnp.maximum(i - 1, 0), own_span, :]).astype(f32)
        down = jnp.where(
            i == cx - 1, halos[1, offset % G, span, :], tile[jnp.minimum(i + 1, cx - 1), own_span, :]).astype(f32)
        return own, ((down - up) * 0.5).astype(bf16)

    def pass_on(step):
        for way in range(2):
            offset = -(step - 1) if way == 0 else step - 1
            span = raw_half[1 - way] if step == 3 else raw_half[way]
            target = pass3 if step == 3 else pass4
            for c in range(CAP):
                i = picked(at(offset), along(way)[0], c)
                own, grad_x = raw_pair(offset, i, span)
                target[way, c, 0] = own
                target[way, c, 1] = grad_x
            send(way, passed(way, step))

    def with_border(own, corners, prior, following):
        ends = (jnp.where((depth == following) & (column == LANES - 1), 0.5, 0.0)
                - jnp.where((depth == prior) & (column == 0), 0.5, 0.0)).astype(bf16)
        return jnp.dot(
            jnp.concatenate([own, corners], axis=1), jnp.concatenate([band[0], ends], axis=0),
            preferred_element_type=f32).astype(bf16)

    def joined(a, b):
        return jnp.concatenate([a, b], axis=0)

    def keep(offset, pair, corners):
        h = at(offset)
        for c in range(CAP):
            i = picked(h, me, c)
            own, grad_x = pair(h, c)
            grad_y = with_border(own, corners, 16 * (h - 1) + 8 + i, 16 * (h + 1) + i)
            whole = jnp.concatenate([own, grad_x, grad_y], axis=1)
            tiles[CAP * h + c] = whole

    def asked_to_smem(way):
        return pltpu.make_async_copy(asked.at[1 - way], asked_s.at[1 - way], local_sem.at[G + way])

    def serve(way):
        asked_to_smem(way).wait()
        for k in range(NBR):
            stage[way, k] = pairs[asked_s[1 - way, 0, way * NBR + k]]
            near_copy(way, k).start()

    def send_fringe(way):
        row = lax.broadcasted_iota(jnp.int32, (32, LANES), 0)
        place = lax.broadcasted_iota(jnp.int32, (32, LANES), 1)
        chosen = jnp.zeros((32, LANES), f32)
        for k, slot in enumerate([asked_s[1 - way, 0, way * NBR + k] for k in range(NBR)] + far):
            h = lax.shift_right_logical(slot, 1)
            i = picked(h, me, slot - 2 * h)
            chosen = jnp.where((row == 2 * k) & (place == 16 * (h - 1) + 8 + i), 1.0, chosen)
            chosen = jnp.where((row == 2 * k + 1) & (place == 16 * (h + 1) + i), 1.0, chosen)
        fringe_out[way] = jnp.dot(
            chosen.astype(bf16), edges[...].reshape(G * 16, channels), preferred_element_type=f32).astype(bf16)
        fringe_copy(way).start()

    everything = pl.ds(0, channels)

    def early_tiles():
        for offset in (0, -1, 1):
            halos_arrived(offset)
            to_smem(offset).wait()
        for offset in (0, -1, 1, -2, 2):
            for c in range(CAP):
                h = at(offset)
                own, grad_x = raw_pair(offset, picked(h, me, c), everything)
                pairs[CAP * h + c, 0] = own
                pairs[CAP * h + c, 1] = grad_x
        for way in range(2):
            @pl.when(there[way])
            def _(way=way):
                serve(way)

    for step in range(1, 5):
        ways = (0, 1) if step < 4 else (0,)
        for way in ways:
            note_copy(way, step, True).wait_recv()
            edge_copy(way, step, True).wait_recv()
            if step < 3 or (step == 3 and way == 0):
                note_copy(way, step + 1).start()
                edge_copy(way, step + 1).start()
            to_smem(-step if way == 0 else step).start()
        if step == 4:
            break
        if step == 2:
            for way in range(2):
                @pl.when(there[way])
                def _(way=way):
                    ask(1 - way).wait_recv()
                    asked_to_smem(way).start()
        for c in ORDER:
            if step == 3 and c == ORDER[2]:
                early_tiles()
            for way in range(2):
                ring(way, step, c).wait_recv()
                if step < 3:
                    send(way, ring(way, step + 1, c))
                offset = -step if way == 0 else step
                if c == 0:
                    send_halo(1, offset)
                if c == 7:
                    send_halo(0, offset)
        if step >= 2:
            for offset in (-step, step):
                halos_arrived(offset)
                to_smem(offset).wait()
            pass_on(step + 1)
        if step == 3:
            for way, offset in ((0, -3), (1, 3)):
                for c in range(CAP):
                    own, grad_x = raw_pair(offset, picked(at(offset), me, c), raw_half[way])
                    raw3[way, c, 0] = own
                    raw3[way, c, 1] = grad_x
                send_late(0, way)

    to_smem(-4).wait()
    for chain in range(2):
        passed(chain, 3).wait_recv()
        send_late(1, chain)
    for way in range(2):
        @pl.when(there[way])
        def _(way=way):
            send_fringe(way)
    corners = transposed(edges[...].reshape(G * 16, channels), band[1])
    for offset in (0, -1, 1, -2, 2):
        keep(offset, lambda h, c: (pairs[CAP * h + c, 0], pairs[CAP * h + c, 1]), corners)
    keep(-3, lambda h, c: tuple(joined(raw3[0, c, p], got3[0, c, p]) for p in range(2)), corners)
    keep(3, lambda h, c: tuple(joined(got3[1, c, p], raw3[1, c, p]) for p in range(2)), corners)
    for chain in range(2):
        passed(chain, 4).wait_recv()
        send_late(2, chain)
    keep(4, lambda h, c: tuple(joined(got4[0, c, p], got4[1, c, p]) for p in range(2)), corners)

    def from_neighbour(way, k, own, grad_x, sides):
        grad_y = with_border(own, sides, 32 * way + 2 * k, 32 * way + 2 * k + 1)
        return jnp.concatenate([own, grad_x, grad_y], axis=1)

    for way in range(2):
        @pl.when(there[1 - way])
        def _(way=way):
            fringe_copy(way).wait_recv()
            for k in range(NBR):
                near_copy(way, k).wait_recv()
    sides = transposed(fringe[...], band[1])
    for way in range(2):
        @pl.when(there[1 - way])
        def _(way=way):
            for k in range(NBR):
                tiles[EARLY + way * NBR + k] = from_neighbour(way, k, near[way, k, 0], near[way, k, 1], sides)
    w_copy.wait()

    def late_tile(way, offset, c):
        halves = {-3: ((0, 0), (1, 0)), 3: ((1, 1), (0, 1)), 4: ((2, 0), (2, 1))}[offset]
        own, grad_x = (joined(*[late[way, kind, chain, c, p] for kind, chain in halves]) for p in range(2))
        k = CAP * LAST.index(offset) + c
        tiles[LATE + way * len(far) + k] = from_neighbour(way, NBR + k, own, grad_x, sides)

    for kinds, offsets in (((0, 1), (-3, 3)), ((2,), (4,))):
        for way in range(2):
            @pl.when(there[1 - way])
            def _(way=way):
                for kind in kinds:
                    for chain in range(2):
                        late_copy(way, kind, chain).wait_recv()
                for offset in offsets:
                    for c in range(CAP):
                        late_tile(way, offset, c)

    def multiply(part, start):
        for k in range(4):
            part[k] = jnp.dot(tiles[place_s[start + k]], weights[start + k], preferred_element_type=f32)

    def add(part, start, live):
        mine = [[((ocn_ref[start + k] == t) & live).astype(f32) for k in range(4)] for t in range(OCN)]
        for strip in range(channels // 16):
            here = pl.ds(16 * strip, 16)
            values = [part[k, here, :] for k in range(4)]
            for t in range(OCN):
                total = sums[t, here, :]
                for k in range(4):
                    total = total + values[k] * mine[t][k]
                sums[t, here, :] = total

    part_b[...] = jnp.zeros(part_b.shape, f32)
    sums[...] = jnp.zeros(sums.shape, f32)

    @pl.loop(0, blocks // 8)
    def _(eight):
        start = eight * 8
        multiply(part_a, start)
        add(part_b, jnp.maximum(start - 4, 0), eight > 0)
        multiply(part_b, start + 4)
        add(part_a, start, True)

    add(part_b, blocks - 4, True)
    for t in range(OCN):
        out_ref[:, t * LANES:(t + 1) * LANES] = sums[t].astype(bf16)

    for way in range(2):
        for copy in under_way[way]:
            copy.wait_send()
        for step in range(1, 5 - way):
            note_copy(way, step).wait_send()
            edge_copy(way, step).wait_send()

        @pl.when(there[way])
        def _(way=way):
            ask(way).wait_send()
            for offset in rows:
                halo(way, offset).wait_send()
            for k in range(NBR):
                near_copy(way, k).wait_send()
            fringe_copy(way).wait_send()
            for kind in range(3):
                for chain in range(2):
                    late_copy(way, kind, chain).wait_send()


def solution(mesh):
    regions = mesh.shape["reg"]

    def per_device(field, send_pick, blk_src, blk_ocn, blk_weight):
        channels, cx, cells = field.shape
        blocks = blk_src.shape[0]
        half = channels // 2
        dma = pltpu.SemaphoreType.DMA
        bf16, f32, i32 = jnp.bfloat16, jnp.float32, jnp.int32
        operands = [
            pltpu.with_memory_space_constraint(x, pltpu.HBM) for x in (field, send_pick, blk_src, blk_ocn, blk_weight)
        ]
        return pl.pallas_call(
            functools.partial(kernel, regions),
            out_shape=jax.ShapeDtypeStruct((channels, OCN * cells), bf16),
            in_specs=[pl.BlockSpec(memory_space=pl.ANY)] * 5,
            out_specs=pl.BlockSpec(memory_space=pltpu.VMEM),
            scratch_shapes=[
                pltpu.VMEM(field.shape, bf16),
                pltpu.SMEM(send_pick.shape, i32),
                pltpu.SMEM(blk_src.shape, i32),
                pltpu.SMEM(blk_ocn.shape, i32),
                pltpu.VMEM((cx, channels, cells), bf16),
                pltpu.VMEM((cx, channels, cells), bf16),
                pltpu.VMEM((cx, channels, cells), bf16),
                pltpu.VMEM((cx, half, cells), bf16),
                pltpu.VMEM((cx, half, cells), bf16),
                pltpu.VMEM((cx, channels, cells), bf16),
                pltpu.VMEM((cx, channels, cells), bf16),
                pltpu.VMEM((2, G, channels, cells), bf16),
                pltpu.VMEM((G, 16, channels), bf16),
                pltpu.VMEM((8, LANES), i32),
                pltpu.VMEM((LANES, channels), bf16),
                pltpu.VMEM((2, CAP, 2, half, cells), bf16),
                pltpu.VMEM((2, CAP, 2, half, cells), bf16),
                pltpu.VMEM((2, CAP, 2, half, cells), bf16),
                pltpu.VMEM((2, CAP, 2, half, cells), bf16),
                pltpu.VMEM((2, CAP, 2, half, cells), bf16),
                pltpu.VMEM((OWN, 2, channels, cells), bf16),
                pltpu.VMEM((SLOTS, channels, 3 * cells), bf16),
                pltpu.VMEM((2, NBR, 2, channels, cells), bf16),
                pltpu.VMEM((2, NBR, 2, channels, cells), bf16),
                pltpu.VMEM((2, 3, 2, CAP, 2, half, cells), bf16),
                pltpu.VMEM((blocks, 3 * cells, cells), bf16),
                pltpu.VMEM((channels * cx, cells), f32),
                pltpu.VMEM((G, 8, LANES), i32),
                pltpu.VMEM((2, 8, LANES), i32),
                pltpu.SMEM((G, 8, LANES), i32),
                pltpu.SMEM((2, 8, LANES), i32),
                pltpu.SMEM((blocks,), i32),
                pltpu.VMEM((2, LANES, LANES), bf16),
                pltpu.VMEM((4, channels, cells), f32),
                pltpu.VMEM((4, channels, cells), f32),
                pltpu.VMEM((OCN, channels, cells), f32),
                pltpu.VMEM((2, 32, channels), bf16),
                dma((2, 3, 8)), dma((2, 3, 8)),
                dma((2, 2)), dma((2, 2)),
                dma((2, 4)), dma((2, 4)),
                dma((2, 4)), dma((2, 4)),
                dma((2, G)), dma((2, G)),
                dma((2,)), dma((2,)),
                dma((2, NBR)), dma((2, NBR)),
                dma((2,)), dma((2,)),
                dma((2, 3, 2)), dma((2, 3, 2)),
                dma((G + 2,)),
                dma((4,)),
                dma,
            ],
            compiler_params=pltpu.CompilerParams(
                collective_id=0, has_side_effects=True, vmem_limit_bytes=VMEM_LIMIT
            ),
            cost_estimate=pl.CostEstimate(
                flops=2 * blocks * channels * 3 * cells * cells, bytes_accessed=4 * 1024 * 1024, transcendentals=0
            ),
        )(*operands)

    placed = (
        P(None, "reg", "grp"),
        P(("grp", "reg")),
        P(("grp", "reg")),
        P(("grp", "reg")),
        P(("grp", "reg"), None, None),
    )
    return jax.shard_map(
        per_device, mesh=mesh, in_specs=placed, out_specs=P(None, ("grp", "reg")), check_vma=False
    )
```

```python
import functools

import jax
import jax.numpy as jnp
from jax import lax
from jax.experimental import pallas as pl
from jax.experimental.pallas import tpu as pltpu
from jax.sharding import PartitionSpec as P

MESH = pl.DeviceIdType.MESH
OCN = 4
CAP = 2
NBR = 4
G = 8
LANES = 128
VMEM_LIMIT = 48 * 1024 * 1024
ORDER = (0, 7, 1, 2, 3, 4, 5, 6)
DEPTH = 5
OWN = G * CAP
EARLY, LATE = OWN, OWN + 2 * NBR
LAST = (-3, 3, 4)
SLOTS = LATE + 2 * CAP * len(LAST)


def transposed(matrix, unit):
    return lax.dot_general(
        unit, matrix, (((1,), (1,)), ((), ())), preferred_element_type=jnp.float32
    ).astype(jnp.bfloat16)


def distinct(src_ref, low):
    found = [jnp.int32(0)] * NBR
    count = jnp.int32(0)
    for b in range(src_ref.shape[0]):
        slot = src_ref[b] - low
        fresh = (slot >= 0) & (slot < OWN)
        for k in range(NBR):
            fresh = fresh & ((count <= k) | (found[k] != slot))
        for k in range(NBR):
            found[k] = jnp.where(fresh & (count == k), slot, found[k])
        count = count + fresh.astype(jnp.int32)
    return found


def kernel(regions, field_hbm, pick_hbm, src_hbm, ocn_hbm, w_hbm, out_ref,
           field_ref, pick_ref, src_ref, ocn_ref,
           row0, row1, row2, row3, row5, row6, row7, halos, edges, wish, fringe,
           pass3, pass4, got3, got4, raw3, pairs, tiles, stage, near, late, weights, flat,
           meta, asked, meta_s, asked_s, place_s, band, part_a, part_b, sums, fringe_out,
           ring_send, ring_recv, pass_send, pass_recv, meta_send, meta_recv, edge_send, edge_recv,
           halo_send, halo_recv, ask_send, ask_recv, near_send, near_recv, fringe_send, fringe_recv,
           late_send, late_recv, local_sem, in_sem, w_sem):
    me = lax.axis_index("grp")
    r = lax.axis_index("reg")
    rows = {0: row0, 1: row1, 2: row2, 3: row3, -3: row5, -2: row6, -1: row7}
    channels, cx = field_ref.shape[:2]
    half = channels // 2
    first, second = pl.ds(0, half), pl.ds(half, half)
    raw_half = (first, second)
    blocks = src_ref.shape[0]
    f32, bf16 = jnp.float32, jnp.bfloat16
    right, left = lax.rem(me + 1, G), lax.rem(me + G - 1, G)
    has_low, has_high = r > 0, r < regions - 1
    low, high = jnp.maximum(r - 1, 0), jnp.minimum(r + 1, regions - 1)
    there = (has_high, has_low)

    def at(offset):
        return lax.rem(me + offset + G, G)

    def along(way):
        return (right if way == 0 else left, r)

    def across(way):
        return (me, high if way == 0 else low)

    def remote(source, target, send, receive, device):
        return pltpu.make_async_remote_copy(
            src_ref=source, dst_ref=target, send_sem=send, recv_sem=receive, device_id=device, device_id_type=MESH)

    arriving = [
        pltpu.make_async_copy(origin, here, in_sem.at[k])
        for k, (origin, here) in enumerate(
            ((field_hbm, field_ref), (pick_hbm, pick_ref), (src_hbm, src_ref), (ocn_hbm, ocn_ref)))
    ]
    for copy in arriving:
        copy.start()
    barrier = pltpu.get_barrier_semaphore()
    for way in range(2):
        pl.semaphore_signal(barrier, inc=1, device_id=along(way), device_id_type=MESH)

    for way in range(2):
        @pl.when(there[way])
        def _(way=way):
            pl.semaphore_signal(barrier, inc=1, device_id=across(way), device_id_type=MESH)

    w_copy = pltpu.make_async_copy(w_hbm, weights, w_sem)
    w_copy.start()

    fringe[...] = jnp.zeros(fringe.shape, bf16)
    for offset in LAST:
        for c in range(CAP):
            pairs[CAP * at(offset) + c] = jnp.zeros(pairs.shape[1:], bf16)

    for way in range(2):
        @pl.when(jnp.logical_not(there[1 - way]))
        def _(way=way):
            for d in range(G):
                halos[way, d] = jnp.zeros(halos.shape[2:], bf16)
            for k in range(NBR):
                tiles[EARLY + way * NBR + k] = jnp.zeros(tiles.shape[1:], bf16)
            for k in range(CAP * len(LAST)):
                tiles[LATE + way * CAP * len(LAST) + k] = jnp.zeros(tiles.shape[1:], bf16)

    arriving[0].wait()
    flat[...] = field_ref[...].astype(f32).reshape(flat.shape)
    for i in range(cx):
        row0[i] = flat[pl.ds(i, channels, stride=cx), :].astype(bf16)

    pl.semaphore_wait(barrier, 2 + has_low.astype(jnp.int32) + has_high.astype(jnp.int32))

    def ring(way, step, c):
        sign = -1 if way == 0 else 1
        source = rows[sign * (step - 1)].at[pl.ds(c, 1)]
        if step == 3:
            source = rows[sign * 2].at[pl.ds(c, 1), raw_half[way]]
        return remote(source, rows[sign * step].at[pl.ds(c, 1)],
                      ring_send.at[way, step - 1, c], ring_recv.at[way, step - 1, c], along(way))

    def passed(way, step, c):
        source, target = (pass3, got3) if step == 3 else (pass4, got4)
        return remote(source.at[way, c], target.at[way, c],
                      pass_send.at[way, step - 3, c], pass_recv.at[way, step - 3, c], along(way))

    def note_copy(way, step, receiving=False):
        sign = -1 if way == 0 else 1
        h = at(sign * (step if receiving else step - 1))
        return remote(meta.at[h], meta.at[h], meta_send.at[way, step - 1], meta_recv.at[way, step - 1], along(way))

    def edge_copy(way, step, receiving=False):
        sign = -1 if way == 0 else 1
        h = at(sign * (step if receiving else step - 1))
        return remote(edges.at[h], edges.at[h], edge_send.at[way, step - 1], edge_recv.at[way, step - 1], along(way))

    def to_smem(offset):
        h = at(offset)
        return pltpu.make_async_copy(meta.at[h], meta_s.at[h], local_sem.at[offset % G])

    def halo(way, offset):
        source = rows[offset].at[cx - 1 if way == 0 else 0]
        target = halos.at[way, offset % G]
        if abs(offset) == 3:
            target = halos.at[way, offset % G, first if offset < 0 else second]
        return remote(source, target, halo_send.at[way, offset % G], halo_recv.at[way, offset % G], across(way))

    def send_halo(way, offset):
        @pl.when(there[way])
        def _():
            halo(way, offset).start()

    def halos_arrived(offset):
        for way in range(2):
            @pl.when(there[1 - way])
            def _(way=way):
                halo(way, offset).wait_recv()

    def ask(way):
        return remote(wish, asked.at[way], ask_send.at[way], ask_recv.at[way], across(way))

    def near_copy(way, k):
        return remote(stage.at[way, k], near.at[way, k], near_send.at[way, k], near_recv.at[way, k], across(way))

    def fringe_copy(way):
        return remote(fringe_out.at[way], fringe.at[pl.ds(32 * way, 32)],
                      fringe_send.at[way], fringe_recv.at[way], across(way))

    def late_copy(way, kind, chain, c):
        return remote((raw3, got3, got4)[kind].at[chain, c], late.at[way, kind, chain, c],
                      late_send.at[way, kind, chain, c], late_recv.at[way, kind, chain, c], across(way))

    def send_late(kind, chain, c):
        for way in range(2):
            @pl.when(there[way])
            def _(way=way):
                late_copy(way, kind, chain, c).start()

    under_way = ([], [])

    def send(way, copy):
        if len(under_way[way]) == DEPTH:
            under_way[way].pop(0).wait_send()
        copy.start()
        under_way[way].append(copy)

    for way in range(2):
        send_halo(way, 0)
    for c in ORDER[:DEPTH]:
        for way in range(2):
            send(way, ring(way, 1, c))

    for copy in arriving[1:]:
        copy.wait()
    lane = lax.broadcasted_iota(jnp.int32, (8, LANES), 1)
    note = jnp.zeros((8, LANES), jnp.int32)
    for k in range(OWN):
        note = jnp.where(lane == k, pick_ref[k], note)
    meta[me] = note
    line = lax.broadcasted_iota(jnp.int32, (16, LANES), 0)
    spot = lax.broadcasted_iota(jnp.int32, (16, LANES), 1)
    border = jnp.zeros((16, channels), f32)
    for i in range(cx):
        chosen = ((line == i) & (spot == 0)) | ((line == 8 + i) & (spot == LANES - 1))
        border = border + lax.dot_general(
            jnp.where(chosen, 1.0, 0.0).astype(bf16), row0[i], (((1,), (1,)), ((), ())), preferred_element_type=f32)
    edges[me] = border.astype(bf16)
    for way in range(2):
        note_copy(way, 1).start()
        edge_copy(way, 1).start()
    to_smem(0).start()
    for c in ORDER[DEPTH:]:
        for way in range(2):
            send(way, ring(way, 1, c))

    wanted = (distinct(src_ref, 0), distinct(src_ref, 2 * OWN))
    request = jnp.zeros((8, LANES), jnp.int32)
    for way in range(2):
        for k in range(NBR):
            request = jnp.where(lane == way * NBR + k, wanted[way][k], request)
    wish[...] = request
    for way in range(2):
        @pl.when(there[way])
        def _(way=way):
            ask(way).start()
    far = [CAP * at(offset) + c for offset in LAST for c in range(CAP)]
    for b in range(blocks):
        slot = src_ref[b]
        found = []
        for way in range(2):
            named = slot - 2 * OWN * way
            where = jnp.int32(EARLY + way * NBR)
            for k in range(1, NBR):
                where = jnp.where(named == wanted[way][k], EARLY + way * NBR + k, where)
            for k, slot_of in enumerate(far):
                where = jnp.where(named == slot_of, LATE + way * len(far) + k, where)
            found.append(where)
        place_s[b] = jnp.where(slot < OWN, found[0], jnp.where(slot < 2 * OWN, slot - OWN, found[1]))

    depth = lax.broadcasted_iota(jnp.int32, (LANES, LANES), 0)
    column = lax.broadcasted_iota(jnp.int32, (LANES, LANES), 1)
    band[0] = (jnp.where(depth == column + 1, 0.5, 0.0) - jnp.where(depth == column - 1, 0.5, 0.0)).astype(bf16)
    band[1] = jnp.where(depth == column, 1.0, 0.0).astype(bf16)

    def picked(h, group, c):
        return meta_s[h, 0, CAP * group + c]

    def raw_pair(offset, i, span):
        tile = rows[offset]
        own_span = pl.ds(0, half) if abs(offset) == 3 else span
        own = tile[i, own_span, :]
        up = jnp.where(i == 0, halos[0, offset % G, span, :], tile[jnp.maximum(i - 1, 0), own_span, :]).astype(f32)
        down = jnp.where(
            i == cx - 1, halos[1, offset % G, span, :], tile[jnp.minimum(i + 1, cx - 1), own_span, :]).astype(f32)
        return own, ((down - up) * 0.5).astype(bf16)

    def pass_on(step):
        for c in range(CAP):
            for way in range(2):
                offset = -(step - 1) if way == 0 else step - 1
                span = raw_half[1 - way] if step == 3 else raw_half[way]
                target = pass3 if step == 3 else pass4
                own, grad_x = raw_pair(offset, picked(at(offset), along(way)[0], c), span)
                target[way, c, 0] = own
                target[way, c, 1] = grad_x
                send(way, passed(way, step, c))

    def with_border(own, corners, prior, following):
        ends = (jnp.where((depth == following) & (column == LANES - 1), 0.5, 0.0)
                - jnp.where((depth == prior) & (column == 0), 0.5, 0.0)).astype(bf16)
        return jnp.dot(
            jnp.concatenate([own, corners], axis=1), jnp.concatenate([band[0], ends], axis=0),
            preferred_element_type=f32).astype(bf16)

    def joined(a, b):
        return jnp.concatenate([a, b], axis=0)

    def keep(offset, pair, corners):
        h = at(offset)
        for c in range(CAP):
            i = picked(h, me, c)
            own, grad_x = pair(h, c)
            grad_y = with_border(own, corners, 16 * (h - 1) + 8 + i, 16 * (h + 1) + i)
            whole = jnp.concatenate([own, grad_x, grad_y], axis=1)
            tiles[CAP * h + c] = whole

    def asked_to_smem(way):
        return pltpu.make_async_copy(asked.at[1 - way], asked_s.at[1 - way], local_sem.at[G + way])

    def serve(way):
        asked_to_smem(way).wait()
        for k in range(NBR):
            stage[way, k] = pairs[asked_s[1 - way, 0, way * NBR + k]]
            near_copy(way, k).start()

    def send_fringe(way):
        row = lax.broadcasted_iota(jnp.int32, (32, LANES), 0)
        place = lax.broadcasted_iota(jnp.int32, (32, LANES), 1)
        chosen = jnp.zeros((32, LANES), f32)
        for k, slot in enumerate([asked_s[1 - way, 0, way * NBR + k] for k in range(NBR)] + far):
            h = lax.shift_right_logical(slot, 1)
            i = picked(h, me, slot - 2 * h)
            chosen = jnp.where((row == 2 * k) & (place == 16 * (h - 1) + 8 + i), 1.0, chosen)
            chosen = jnp.where((row == 2 * k + 1) & (place == 16 * (h + 1) + i), 1.0, chosen)
        fringe_out[way] = jnp.dot(
            chosen.astype(bf16), edges[...].reshape(G * 16, channels), preferred_element_type=f32).astype(bf16)
        fringe_copy(way).start()

    everything = pl.ds(0, channels)

    def early_tiles():
        for offset in (0, -1, 1):
            halos_arrived(offset)
            to_smem(offset).wait()
        for offset in (0, -1, 1, -2, 2):
            for c in range(CAP):
                h = at(offset)
                own, grad_x = raw_pair(offset, picked(h, me, c), everything)
                pairs[CAP * h + c, 0] = own
                pairs[CAP * h + c, 1] = grad_x
        for way in range(2):
            @pl.when(there[way])
            def _(way=way):
                serve(way)

    for step in range(1, 5):
        ways = (0, 1) if step < 4 else (0,)
        for way in ways:
            note_copy(way, step, True).wait_recv()
            edge_copy(way, step, True).wait_recv()
            if step < 3 or (step == 3 and way == 0):
                note_copy(way, step + 1).start()
                edge_copy(way, step + 1).start()
            to_smem(-step if way == 0 else step).start()
        if step == 4:
            break
        if step == 2:
            for way in range(2):
                @pl.when(there[way])
                def _(way=way):
                    ask(1 - way).wait_recv()
                    asked_to_smem(way).start()
        for c in ORDER:
            if step == 3 and c == ORDER[2]:
                early_tiles()
            for way in range(2):
                ring(way, step, c).wait_recv()
                if step < 3:
                    send(way, ring(way, step + 1, c))
                offset = -step if way == 0 else step
                if c == 0:
                    send_halo(1, offset)
                if c == 7:
                    send_halo(0, offset)
        if step >= 2:
            for offset in (-step, step):
                halos_arrived(offset)
                to_smem(offset).wait()
            pass_on(step + 1)
        if step == 3:
            for way, offset in ((0, -3), (1, 3)):
                for c in range(CAP):
                    own, grad_x = raw_pair(offset, picked(at(offset), me, c), raw_half[way])
                    raw3[way, c, 0] = own
                    raw3[way, c, 1] = grad_x
                    send_late(0, way, c)

    to_smem(-4).wait()
    for c in range(CAP):
        for chain in range(2):
            passed(chain, 3, c).wait_recv()
            send_late(1, chain, c)
    for way in range(2):
        @pl.when(there[way])
        def _(way=way):
            send_fringe(way)
    corners = transposed(edges[...].reshape(G * 16, channels), band[1])
    for offset in (0, -1, 1, -2, 2):
        keep(offset, lambda h, c: (pairs[CAP * h + c, 0], pairs[CAP * h + c, 1]), corners)
    keep(-3, lambda h, c: tuple(joined(raw3[0, c, p], got3[0, c, p]) for p in range(2)), corners)
    keep(3, lambda h, c: tuple(joined(got3[1, c, p], raw3[1, c, p]) for p in range(2)), corners)
    for c in range(CAP):
        for chain in range(2):
            passed(chain, 4, c).wait_recv()
            send_late(2, chain, c)
    keep(4, lambda h, c: tuple(joined(got4[0, c, p], got4[1, c, p]) for p in range(2)), corners)

    def from_neighbour(way, k, own, grad_x, sides):
        grad_y = with_border(own, sides, 32 * way + 2 * k, 32 * way + 2 * k + 1)
        return jnp.concatenate([own, grad_x, grad_y], axis=1)

    for way in range(2):
        @pl.when(there[1 - way])
        def _(way=way):
            fringe_copy(way).wait_recv()
            for k in range(NBR):
                near_copy(way, k).wait_recv()
    sides = transposed(fringe[...], band[1])
    for way in range(2):
        @pl.when(there[1 - way])
        def _(way=way):
            for k in range(NBR):
                tiles[EARLY + way * NBR + k] = from_neighbour(way, k, near[way, k, 0], near[way, k, 1], sides)
    w_copy.wait()

    def late_tile(way, offset, c):
        halves = {-3: ((0, 0), (1, 0)), 3: ((1, 1), (0, 1)), 4: ((2, 0), (2, 1))}[offset]
        own, grad_x = (joined(*[late[way, kind, chain, c, p] for kind, chain in halves]) for p in range(2))
        k = CAP * LAST.index(offset) + c
        tiles[LATE + way * len(far) + k] = from_neighbour(way, NBR + k, own, grad_x, sides)

    for kinds, offsets in (((0, 1), (-3, 3)), ((2,), (4,))):
        for way in range(2):
            @pl.when(there[1 - way])
            def _(way=way):
                for kind in kinds:
                    for chain in range(2):
                        for c in range(CAP):
                            late_copy(way, kind, chain, c).wait_recv()
                for offset in offsets:
                    for c in range(CAP):
                        late_tile(way, offset, c)

    def multiply(part, start):
        for k in range(4):
            part[k] = jnp.dot(tiles[place_s[start + k]], weights[start + k], preferred_element_type=f32)

    def add(part, start, live):
        mine = [[((ocn_ref[start + k] == t) & live).astype(f32) for k in range(4)] for t in range(OCN)]
        for strip in range(channels // 16):
            here = pl.ds(16 * strip, 16)
            values = [part[k, here, :] for k in range(4)]
            for t in range(OCN):
                total = sums[t, here, :]
                for k in range(4):
                    total = total + values[k] * mine[t][k]
                sums[t, here, :] = total

    part_b[...] = jnp.zeros(part_b.shape, f32)
    sums[...] = jnp.zeros(sums.shape, f32)

    for start in range(0, blocks, 8):
        multiply(part_a, start)
        if start > 0:
            add(part_b, start - 4, True)
        multiply(part_b, start + 4)
        add(part_a, start, True)

    add(part_b, blocks - 4, True)
    for t in range(OCN):
        out_ref[:, t * LANES:(t + 1) * LANES] = sums[t].astype(bf16)

    for way in range(2):
        for copy in under_way[way]:
            copy.wait_send()
        for step in range(1, 5 - way):
            note_copy(way, step).wait_send()
            edge_copy(way, step).wait_send()

        @pl.when(there[way])
        def _(way=way):
            ask(way).wait_send()
            for offset in rows:
                halo(way, offset).wait_send()
            for k in range(NBR):
                near_copy(way, k).wait_send()
            fringe_copy(way).wait_send()
            for kind in range(3):
                for chain in range(2):
                    for c in range(CAP):
                        late_copy(way, kind, chain, c).wait_send()


def solution(mesh):
    regions = mesh.shape["reg"]

    def per_device(field, send_pick, blk_src, blk_ocn, blk_weight):
        channels, cx, cells = field.shape
        blocks = blk_src.shape[0]
        half = channels // 2
        dma = pltpu.SemaphoreType.DMA
        bf16, f32, i32 = jnp.bfloat16, jnp.float32, jnp.int32
        operands = [
            pltpu.with_memory_space_constraint(x, pltpu.HBM) for x in (field, send_pick, blk_src, blk_ocn, blk_weight)
        ]
        return pl.pallas_call(
            functools.partial(kernel, regions),
            out_shape=jax.ShapeDtypeStruct((channels, OCN * cells), bf16),
            in_specs=[pl.BlockSpec(memory_space=pl.ANY)] * 5,
            out_specs=pl.BlockSpec(memory_space=pltpu.VMEM),
            scratch_shapes=[
                pltpu.VMEM(field.shape, bf16),
                pltpu.SMEM(send_pick.shape, i32),
                pltpu.SMEM(blk_src.shape, i32),
                pltpu.SMEM(blk_ocn.shape, i32),
                pltpu.VMEM((cx, channels, cells), bf16),
                pltpu.VMEM((cx, channels, cells), bf16),
                pltpu.VMEM((cx, channels, cells), bf16),
                pltpu.VMEM((cx, half, cells), bf16),
                pltpu.VMEM((cx, half, cells), bf16),
                pltpu.VMEM((cx, channels, cells), bf16),
                pltpu.VMEM((cx, channels, cells), bf16),
                pltpu.VMEM((2, G, channels, cells), bf16),
                pltpu.VMEM((G, 16, channels), bf16),
                pltpu.VMEM((8, LANES), i32),
                pltpu.VMEM((LANES, channels), bf16),
                pltpu.VMEM((2, CAP, 2, half, cells), bf16),
                pltpu.VMEM((2, CAP, 2, half, cells), bf16),
                pltpu.VMEM((2, CAP, 2, half, cells), bf16),
                pltpu.VMEM((2, CAP, 2, half, cells), bf16),
                pltpu.VMEM((2, CAP, 2, half, cells), bf16),
                pltpu.VMEM((OWN, 2, channels, cells), bf16),
                pltpu.VMEM((SLOTS, channels, 3 * cells), bf16),
                pltpu.VMEM((2, NBR, 2, channels, cells), bf16),
                pltpu.VMEM((2, NBR, 2, channels, cells), bf16),
                pltpu.VMEM((2, 3, 2, CAP, 2, half, cells), bf16),
                pltpu.VMEM((blocks, 3 * cells, cells), bf16),
                pltpu.VMEM((channels * cx, cells), f32),
                pltpu.VMEM((G, 8, LANES), i32),
                pltpu.VMEM((2, 8, LANES), i32),
                pltpu.SMEM((G, 8, LANES), i32),
                pltpu.SMEM((2, 8, LANES), i32),
                pltpu.SMEM((blocks,), i32),
                pltpu.VMEM((2, LANES, LANES), bf16),
                pltpu.VMEM((4, channels, cells), f32),
                pltpu.VMEM((4, channels, cells), f32),
                pltpu.VMEM((OCN, channels, cells), f32),
                pltpu.VMEM((2, 32, channels), bf16),
                dma((2, 3, 8)), dma((2, 3, 8)),
                dma((2, 2, CAP)), dma((2, 2, CAP)),
                dma((2, 4)), dma((2, 4)),
                dma((2, 4)), dma((2, 4)),
                dma((2, G)), dma((2, G)),
                dma((2,)), dma((2,)),
                dma((2, NBR)), dma((2, NBR)),
                dma((2,)), dma((2,)),
                dma((2, 3, 2, CAP)), dma((2, 3, 2, CAP)),
                dma((G + 2,)),
                dma((4,)),
                dma,
            ],
            compiler_params=pltpu.CompilerParams(
                collective_id=0, has_side_effects=True, vmem_limit_bytes=VMEM_LIMIT
            ),
            cost_estimate=pl.CostEstimate(
                flops=2 * blocks * channels * 3 * cells * cells, bytes_accessed=4 * 1024 * 1024, transcendentals=0
            ),
        )(*operands)

    placed = (
        P(None, "reg", "grp"),
        P(("grp", "reg")),
        P(("grp", "reg")),
        P(("grp", "reg")),
        P(("grp", "reg"), None, None),
    )
    return jax.shard_map(
        per_device, mesh=mesh, in_specs=placed, out_specs=P(None, ("grp", "reg")), check_vma=False
    )
```
